512 devices in a mesh: tm: 32 (over x, z), row: 8 (over y), col: 2 (over core).
Axes of the slice: x: 4, y: 8, z: 8, core: 2. Of those that a mesh axis runs over, the one named last changes fastest.
Arguments:
- features: bfloat16 [64, 48, 32, 512], P('tm', 'row', 'col'), may hold values from -16 to 16, as said below
- gn1_gain: float32 [512], replicated, may hold values from 0.1 to 1.9
- gn1_bias: float32 [512], replicated, may hold values from -3 to 3
- conv1_weight: bfloat16 [27, 512, 256], P(None, ('row', 'col')), may hold values from -0.0546875 to 0.0546875
- conv1_bias: float32 [256], replicated, may hold values from -3 to 3
- skip_weight: bfloat16 [1, 512, 256], P(None, ('row', 'col')), may hold values from -0.25 to 0.25
- gn2_gain: float32 [256], replicated, may hold values from 0.1 to 1.9
- gn2_bias: float32 [256], replicated, may hold values from -3 to 3
- conv2_weight: bfloat16 [27, 256, 256], P(None, ('row', 'col')), may hold values from -0.078125 to 0.078125
- conv2_bias: float32 [256], replicated, may hold values from -3 to 3
Outputs:
- block_out: bfloat16 [64, 48, 32, 256], P('tm', 'row', 'col')
The draws below stay inside these ranges and needn't reach their ends.
Inputs may be any that keep to these rules, and one draw needn't show every extreme that they name: Latent features of the decoder, of mixed scales over frames, positions and channels.
All inputs are finite; a program needn't handle non-finite values.
Results may differ from the reference program's by a relative error of at most 0.0065.
Values may be sent and summed in bfloat16 or wider, within the bound.
No kernel may reach another device: no remote copies, remote signals or barrier semaphores. Data moves between devices by JAX's collectives and lax.ppermute only.
A program may use at most 64 MiB of HBM per device.

```python
import jax
import jax.numpy as jnp
from jax import lax

C_IN = 512
C_OUT = 256
GROUPS = 32
NT = 64
NH = 48
NW = 32


def draw_features(key, part):
    key = jax.random.fold_in(key, 11)
    keys = jax.random.split(key, 8)
    frame = jnp.arange(NT, dtype=jnp.float32) / float(max(NT - 1, 1))
    rise = jnp.exp(jnp.log(3.0) * frame) * jnp.exp(jax.random.uniform(keys[0], (NT,), jnp.float32, -0.2, 0.2))
    rows = jnp.exp(jax.random.uniform(keys[1], (NH,), jnp.float32, 0.0, jnp.log(3.0)))
    halves = jnp.arange(NW, dtype=jnp.int32) * 2 // NW
    pick = jax.random.randint(keys[6], (), 0, 2, dtype=jnp.int32)
    step = jnp.where(halves == pick, 2.5, 1.0).astype(jnp.float32)
    cols = jnp.exp(jax.random.uniform(keys[2], (NW,), jnp.float32, 0.0, jnp.log(3.0))) * step
    offsets = 0.8 * jax.random.normal(keys[7], (2, C_IN), jnp.float32)
    placed = jnp.where(halves[:, None] == 0, offsets[0][None, :], offsets[1][None, :])
    chan = jnp.exp(jax.random.uniform(keys[3], (C_IN,), jnp.float32, 0.0, jnp.log(10.0)))
    noise = jnp.clip(jax.random.normal(keys[4], (NT, NH, NW, C_IN), jnp.float32), -4.0, 4.0)
    noise = noise + placed[None, None, :, :]
    scale = 0.035 * rise[:, None, None, None] * rows[None, :, None, None] * cols[None, None, :, None] * chan
    return jnp.clip(scale * noise, -16.0, 16.0).astype(jnp.bfloat16)


def shard_levels(stream_key, extent, cuts, least, high):
    level = 1.0
    for axis_at, shards_of in cuts:
        draws = jax.random.uniform(jax.random.fold_in(jax.random.fold_in(stream_key, 6), axis_at), (shards_of,), jnp.float32, least / len(cuts), high / len(cuts))
        level = level * jnp.repeat(jnp.exp(draws), extent[axis_at] // shards_of).reshape((-1,) + (1,) * (len(extent) - 1 - axis_at))
    return level


def bell_draw(rng, extent, width, limit, pieces=(), held_as=jnp.bfloat16):
    array = width * jax.random.normal(rng, extent, jnp.float32)
    if pieces:
        array = array * shard_levels(rng, extent, pieces, -0.22, 0.18)
    return jnp.clip(array, -limit, limit).astype(held_as)


def setup_inputs(seed: int = 0) -> dict:
    arg_keys = jax.random.split(jax.random.key(seed), 11)
    features = draw_features(jax.random.fold_in(arg_keys[10], 71), 0)
    gn1_gain = jnp.clip(1.0 + 0.18 * jax.random.normal(arg_keys[1], (C_IN,), jnp.float32), 0.1, 1.9)
    gn1_bias = bell_draw(arg_keys[2], (C_IN,), 0.5, 3.0, (), jnp.float32)
    conv1_weight = bell_draw(arg_keys[3], (27, C_IN, C_OUT), (27 * C_IN) ** -0.5, 0.0546875, ((1, 16),))
    conv1_bias = bell_draw(arg_keys[4], (C_OUT,), 0.5, 3.0, (), jnp.float32)
    skip_weight = bell_draw(arg_keys[5], (1, C_IN, C_OUT), C_IN ** -0.5, 0.25, ((1, 16),))
    gn2_gain = jnp.clip(1.0 + 0.18 * jax.random.normal(arg_keys[6], (C_OUT,), jnp.float32), 0.1, 1.9)
    gn2_bias = bell_draw(arg_keys[7], (C_OUT,), 0.5, 3.0, (), jnp.float32)
    conv2_weight = bell_draw(arg_keys[8], (27, C_OUT, C_OUT), (27 * C_OUT) ** -0.5, 0.078125, ((1, 16),))
    conv2_bias = bell_draw(arg_keys[9], (C_OUT,), 0.5, 3.0, (), jnp.float32)
    return dict(features=features, gn1_gain=gn1_gain, gn1_bias=gn1_bias, conv1_weight=conv1_weight, conv1_bias=conv1_bias, skip_weight=skip_weight, gn2_gain=gn2_gain, gn2_bias=gn2_bias, conv2_weight=conv2_weight, conv2_bias=conv2_bias)


def group_silu(values, gain, shift):
    chans = values.shape[-1]
    grouped = values.reshape(-1, GROUPS, chans // GROUPS)
    mean = lax.optimization_barrier(jnp.mean(grouped, axis=(0, 2)))
    centred = grouped - mean[None, :, None]
    spread = lax.optimization_barrier(jnp.mean(centred * centred, axis=(0, 2)))
    normed = centred * jax.lax.rsqrt(spread + 1e-06)[None, :, None]
    normed = normed.reshape(values.shape) * gain + shift
    return jax.nn.silu(normed).astype(jnp.bfloat16)

def causal_conv(field, weight):
    frames, rows, cols, chans = field.shape
    padded = jnp.pad(field, ((2, 0), (1, 1), (1, 1), (0, 0)), mode='edge')
    total = jnp.zeros((frames * rows * cols, weight.shape[2]), jnp.float32)
    for tap in range(27):
        dt, dy, dx = (tap // 9, tap // 3 % 3, tap % 3)
        window = padded[dt:dt + frames, dy:dy + rows, dx:dx + cols].reshape(-1, chans)
        total = total + jnp.dot(window, weight[tap], preferred_element_type=jnp.float32)
    return total

def reference(features, gn1_gain, gn1_bias, conv1_weight, conv1_bias, skip_weight, gn2_gain, gn2_bias, conv2_weight, conv2_bias):
    hidden1 = group_silu(features.astype(jnp.float32), gn1_gain, gn1_bias)
    middle = causal_conv(hidden1, conv1_weight) + conv1_bias
    middle = middle.reshape(NT, NH, NW, C_OUT)
    hidden2 = group_silu(middle, gn2_gain, gn2_bias)
    second = causal_conv(hidden2, conv2_weight) + conv2_bias
    shortcut = jnp.dot(features.reshape(-1, C_IN), skip_weight[0], preferred_element_type=jnp.float32)
    return (shortcut + second).astype(jnp.bfloat16).reshape(NT, NH, NW, C_OUT)
```

```python
import jax
import jax.numpy as jnp
from jax import lax
from jax.sharding import PartitionSpec as P

GROUPS = 32


def moved(block, axis, distance):
    size = lax.axis_size(axis)
    route = [(i, i + distance) for i in range(size) if 0 <= i + distance < size]
    return lax.ppermute(block, axis, route)


def swapped(block, axis):
    return lax.ppermute(block, axis, [(0, 1), (1, 0)])


def spread_to_all(stats, axes, size):
    copies = jnp.broadcast_to(stats[None, None, :], (size, 1, stats.shape[0]))
    return lax.all_to_all(copies, axes, 0, 0, tiled=True)[:, 0]


def merged(parts, count):
    means, squares = parts[:, :GROUPS], parts[:, GROUPS : 2 * GROUPS]
    mean = jnp.mean(means, axis=0)
    off = means - mean[None]
    return mean, jnp.sum(squares, axis=0) + count * jnp.sum(off * off, axis=0)


def local_stats(flat):
    n, c = flat.shape
    per_group = c // GROUPS
    mean = jnp.sum(jnp.sum(flat, axis=0).reshape(GROUPS, per_group), axis=1) / (n * per_group)
    centred = flat - jnp.repeat(mean, per_group)[None]
    squares = jnp.sum(jnp.sum(centred * centred, axis=0).reshape(GROUPS, per_group), axis=1)
    return jnp.concatenate([mean, squares, jnp.zeros((128 - 2 * GROUPS,), jnp.float32)])


def normed_silu(values, mean, squares, total, gain, shift):
    per_group = values.shape[-1] // GROUPS
    scale = lax.rsqrt(squares / total + 1e-06)
    mean, scale = jnp.repeat(mean, per_group), jnp.repeat(scale, per_group)
    normed = (values - mean) * scale * gain + shift
    return jax.nn.silu(normed).astype(jnp.bfloat16)


def conv(padded, weight):
    frames = padded.shape[0] - 2
    weight = weight.reshape(3, 3, 3, *weight.shape[1:])
    total = 0.0
    for dt in range(3):
        total = total + lax.conv_general_dilated(
            padded[dt : dt + frames],
            weight[dt],
            (1, 1),
            "VALID",
            dimension_numbers=("NHWC", "HWIO", "NHWC"),
            preferred_element_type=jnp.float32,
        )
    return total


def per_device(
    features,
    gn1_gain,
    gn1_bias,
    conv1_weight,
    conv1_bias,
    skip_weight,
    gn2_gain,
    gn2_bias,
    conv2_weight,
    conv2_bias,
):
    frames, rows, cols, chans_in = features.shape
    chans_out = conv1_weight.shape[2]
    ntm, nrow, ncol = (lax.axis_size(a) for a in ("tm", "row", "col"))
    tm, row, col = (lax.axis_index(a) for a in ("tm", "row", "col"))
    positions = frames * rows * cols
    plane = nrow * ncol

    first_weight = lax.all_gather(conv1_weight, ("row", "col"), axis=1, tiled=True)
    share = conv2_weight.shape[1]
    halves = skip_weight.reshape(2, share, chans_out)
    later = lax.all_gather(
        jnp.concatenate([conv2_weight, halves], axis=0), ("row", "col"), axis=1, tiled=True
    )
    second_weight = later[:27]
    skip = later[27:].reshape(2, plane, share, chans_out).transpose(1, 0, 2, 3)
    skip = skip.reshape(chans_in, chans_out)

    back_one = moved(features, "tm", 1)
    back_two = moved(features, "tm", 2)
    first_twice = jnp.concatenate([features[:1], features[:1]], axis=0)
    back_one = jnp.where(tm == 0, first_twice, back_one)
    earliest = jnp.concatenate([back_one[:1], back_one[:1]], axis=0)
    back_two = jnp.where(tm <= 1, earliest, back_two)
    volume = jnp.concatenate([back_two, back_one, features], axis=0)

    stats = local_stats(features.reshape(positions, chans_in).astype(jnp.float32))
    count = float(positions * (chans_in // GROUPS))
    mean, squares = merged(spread_to_all(stats, ("row", "col"), plane), count)
    stats = jnp.concatenate([mean, squares, jnp.zeros((128 - 2 * GROUPS,), jnp.float32)])
    mean, squares = merged(spread_to_all(stats, "tm", ntm), count * plane)

    above = moved(volume[:, -2:], "row", 1)
    below = moved(volume[:, :2], "row", -1)
    above = jnp.where(row == 0, volume[:, :1], above)
    below = jnp.where(row == nrow - 1, volume[:, -1:], below)
    volume = jnp.concatenate([above, volume, below], axis=1)
    border = jnp.where(col == 0, volume[:, :, -2:], volume[:, :, :2])
    border = swapped(border, "col")
    left = jnp.where(col == 0, volume[:, :, :1], border)
    right = jnp.where(col == 0, border, volume[:, :, -1:])
    volume = jnp.concatenate([left, volume, right], axis=2)

    hidden1 = normed_silu(
        volume.astype(jnp.float32), mean, squares, count * plane * ntm, gn1_gain, gn1_bias
    )
    middle = conv(hidden1, first_weight) + conv1_bias

    own = middle[2:, 1:-1, 1:-1].reshape(positions, chans_out)
    stats = local_stats(own)
    count = float(positions * (chans_out // GROUPS))
    mean, squares = merged(spread_to_all(stats, ("row", "col"), plane), count)
    stats = jnp.concatenate([mean, squares, jnp.zeros((128 - 2 * GROUPS,), jnp.float32)])
    mean, squares = merged(spread_to_all(stats, "tm", ntm), count * plane)
    hidden2 = normed_silu(middle, mean, squares, count * plane * ntm, gn2_gain, gn2_bias)

    top = jnp.where(row == 0, hidden2[:, 1:2], hidden2[:, :1])
    bottom = jnp.where(row == nrow - 1, hidden2[:, -2:-1], hidden2[:, -1:])
    hidden2 = jnp.concatenate([top, hidden2[:, 1:-1], bottom], axis=1)
    left = jnp.where(col == 0, hidden2[:, :, 1:2], hidden2[:, :, :1])
    right = jnp.where(col == ncol - 1, hidden2[:, :, -2:-1], hidden2[:, :, -1:])
    hidden2 = jnp.concatenate([left, hidden2[:, :, 1:-1], right], axis=2)
    early = jnp.where(tm == 0, hidden2[2:3], hidden2[:2])
    hidden2 = jnp.concatenate([early, hidden2[2:]], axis=0)

    shortcut = jnp.dot(
        features.reshape(positions, chans_in), skip, preferred_element_type=jnp.float32
    )
    second = conv(hidden2, second_weight)
    block_out = shortcut.reshape(second.shape) + second + conv2_bias
    return block_out.astype(jnp.bfloat16)


def solution(mesh):
    in_specs = (
        P("tm", "row", "col", None),
        P(),
        P(),
        P(None, ("row", "col"), None),
        P(),
        P(None, ("row", "col"), None),
        P(),
        P(),
        P(None, ("row", "col"), None),
        P(),
    )
    out_specs = P("tm", "row", "col", None)
    return jax.shard_map(
        per_device, mesh=mesh, in_specs=in_specs, out_specs=out_specs, check_vma=False
    )
```

```python
import functools

import jax
import jax.numpy as jnp
from jax import lax
from jax.experimental import pallas as pl
from jax.experimental.pallas import tpu as pltpu
from jax.sharding import PartitionSpec as P

GROUPS = 32
MIB = 1024 * 1024
VMEM = pltpu.VMEM
SMEM = pltpu.SMEM


def moved(block, axis, distance):
    size = lax.axis_size(axis)
    route = [(i, i + distance) for i in range(size) if 0 <= i + distance < size]
    return lax.ppermute(block, axis, route)


def swapped(block, axis):
    return lax.ppermute(block, axis, [(0, 1), (1, 0)])


def as_rows(row):
    return jnp.concatenate([row[:, 128 * j : 128 * (j + 1)] for j in range(row.shape[1] // 128)], axis=0)


def as_row(rows):
    return jnp.concatenate([rows[j : j + 1] for j in range(rows.shape[0])], axis=1)


def packed(mean, squares):
    half = 4
    mean, squares = as_rows(mean), as_rows(squares)
    if mean.shape[0] < half:
        blank = jnp.zeros((half - mean.shape[0], 128), jnp.float32)
        mean = jnp.concatenate([mean, blank], axis=0)
        squares = jnp.concatenate([squares, blank], axis=0)
    return jnp.concatenate([mean, squares], axis=0)


def merged(parts_ref, count):
    parts = parts_ref[...]
    total = jnp.sum(parts, axis=0)
    mean = total / parts.shape[0]
    off = parts - mean[None]
    between = jnp.sum(off * off, axis=0)
    return jnp.concatenate([mean[:4], total[4:] + count * between[:4]], axis=0)


def group_average(rows, size):
    lane = lax.broadcasted_iota(jnp.int32, rows.shape, 1)
    step = 1
    while step < size:
        up, down = pltpu.roll(rows, 128 - step, 1), pltpu.roll(rows, step, 1)
        rows = rows + jnp.where((lane & step) == 0, up, down)
        step *= 2
    return rows / size


def group_moments(tile, count, size, chans):
    mean, squares = tile[:4], tile[4:]
    centre = group_average(mean, size)
    off = mean - centre
    variance = group_average(squares / count + off * off, size)
    scale = lax.rsqrt(variance + 1e-06)
    k = chans // 128
    return as_row(centre[:k]), as_row(scale[:k])


def silu_of(values, mean, scale, gain, shift):
    return jax.nn.silu((values - mean) * scale * gain + shift)


def channel_stats(values, keep, count):
    if keep is not None:
        mean = jnp.sum(jnp.where(keep, values, 0.0), axis=0, keepdims=True) / count
        off = jnp.where(keep, values - mean, 0.0)
    else:
        mean = jnp.sum(values, axis=0, keepdims=True) / count
        off = values - mean
    return packed(mean, jnp.sum(off * off, axis=0, keepdims=True))


def stats_kernel(x_ref, out_ref):
    values = x_ref[...].astype(jnp.float32)
    tile = channel_stats(values, None, float(values.shape[0]))
    out_ref[...] = jnp.broadcast_to(tile[None], out_ref.shape)


def merge_kernel(count, parts_ref, out_ref):
    out_ref[...] = jnp.broadcast_to(merged(parts_ref, count)[None], out_ref.shape)


def hidden1_kernel(
    count, peers, place_ref, parts_ref, gain_ref, shift_ref, centre_ref, above_ref, below_ref, border_ref, out_ref, plain, side
):
    chans = centre_ref.shape[-1]
    tile = merged(parts_ref, count)
    mean, scale = group_moments(tile, count * peers, chans // GROUPS, chans)
    gain, shift = gain_ref[...], shift_ref[...]
    row, col = place_ref[0], place_ref[1]

    def normed(block):
        return silu_of(block.astype(jnp.float32), mean, scale, gain, shift)

    def put(y, block):
        for j in range(chans // 128):
            plain[j, 16 * y : 16 * y + 16, :] = block[:, 128 * j : 128 * (j + 1)]

    def frame(t, _):
        own = [normed(centre_ref[t, y]) for y in range(6)]
        for y in range(2):
            put(y, jnp.where(row == 0, own[0], normed(above_ref[t, y])))
            put(y + 8, jnp.where(row == 7, own[5], normed(below_ref[t, y])))
        for y in range(6):
            put(y + 2, own[y])
        for x in range(2):
            side[pl.ds(16 * x, 16), :] = normed(border_ref[t, x])
        for dy in range(3):

            def column(x):
                pieces = [plain[j, pl.ds(16 * dy + x, 8, stride=16), :] for j in range(chans // 128)]
                return jnp.concatenate(pieces, axis=1)

            inner = [column(x) for x in range(16)]
            outer = [side[pl.ds(16 * x + dy, 8), :] for x in range(2)]
            left = [jnp.where(col == 0, inner[0], o) for o in outer]
            right = [jnp.where(col == 0, o, inner[15]) for o in outer]
            columns = left + inner + right
            base = pl.multiple_of(t * 160, 16)
            for p in range(2):
                for i in range(10 - p):
                    pair = jnp.concatenate([columns[2 * i + p], columns[2 * i + p + 1]], axis=0)
                    out_ref[2 * dy + p, pl.ds(base + 16 * i, 16), :] = pair.astype(jnp.bfloat16)
            out_ref[2 * dy + 1, pl.ds(base + 144, 16), :] = jnp.zeros((16, chans), jnp.bfloat16)
        return 0

    lax.fori_loop(0, 6, frame, 0)


def conv1_kernel(count, copies_ref, weight_ref, bias_ref, middle_ref, stats_ref):
    dy, dt = pl.program_id(0), pl.program_id(1)

    @pl.when((dy == 0) & (dt == 0))
    def _():
        middle_ref[...] = jnp.broadcast_to(bias_ref[...], middle_ref.shape)

    def window(t, dx):
        start = pl.multiple_of((dt + t) * 160 + (dx // 2) * 16, 16)
        return copies_ref[dx % 2, pl.ds(start, 144), :]

    taps = [jnp.concatenate([window(t, dx) for t in range(4)], axis=0) for dx in range(3)]
    lhs = jnp.concatenate(taps, axis=1)
    weight = weight_ref[...].reshape(lhs.shape[1], weight_ref.shape[2])
    middle_ref[...] += jnp.dot(lhs, weight, preferred_element_type=jnp.float32)

    @pl.when((dy == 2) & (dt == 2))
    def _():
        values = middle_ref[288:, :]
        place = lax.broadcasted_iota(jnp.int32, values.shape, 0)
        y, x = place % 8, (place // 8) % 18
        keep = (y >= 1) & (y <= 6) & (x >= 1) & (x <= 16)
        tile = channel_stats(values, keep, count)
        stats_ref[...] = jnp.broadcast_to(tile[None], stats_ref.shape)


def conv2_kernel(
    count, peers, place_ref, parts_ref, gain_ref, shift_ref, bias_ref, middle_ref, features_ref, weight_ref, skip_a_ref, skip_b_ref,
    out_ref, copies, total
):
    dt = pl.program_id(0)
    chans = middle_ref.shape[1]

    @pl.when(dt == 0)
    def _():
        row, col, tm = place_ref[0], place_ref[1], place_ref[2]
        tile = merged(parts_ref, count)
        mean, scale = group_moments(tile, count * peers, chans // GROUPS, chans)
        gain, shift = gain_ref[...], shift_ref[...]
        y = lax.broadcasted_iota(jnp.int32, (8, chans), 0)
        for t in range(4):
            source = jnp.where((tm == 0) & (t < 2), 2, t) if t < 2 else t
            block = middle_ref[pl.ds(pl.multiple_of(source * 144, 16), 144), :]
            block = silu_of(block, mean, scale, gain, shift)
            columns = [block[8 * x : 8 * x + 8] for x in range(18)]
            columns[0] = jnp.where(col == 0, columns[1], columns[0])
            columns[17] = jnp.where(col == 1, columns[16], columns[17])
            for x in range(18):
                column = columns[x]
                column = jnp.where((y == 0) & (row == 0), pltpu.roll(column, 7, 0), column)
                columns[x] = jnp.where((y == 7) & (row == 7), pltpu.roll(column, 1, 0), column)
            for dy in range(3):
                turned = columns if dy == 0 else [pltpu.roll(c, 8 - dy, 0) for c in columns]
                for p in range(2):
                    for i in range(9 - p):
                        pair = jnp.concatenate([turned[2 * i + p], turned[2 * i + p + 1]], axis=0)
                        copies[2 * dy + p, pl.ds(144 * t + 16 * i, 16), :] = pair.astype(jnp.bfloat16)

    def window(t, dy, dx):
        start = pl.multiple_of((dt + t) * 144 + (dx // 2) * 16, 16)
        return copies[2 * dy + dx % 2, pl.ds(start, 128), :]

    sums = None
    for dy in range(3):
        taps = [jnp.concatenate([window(t, dy, dx) for t in range(2)], axis=0) for dx in range(3)]
        lhs = jnp.concatenate(taps, axis=1)
        weight = weight_ref[3 * dy : 3 * dy + 3].reshape(lhs.shape[1], chans)
        product = jnp.dot(lhs, weight, preferred_element_type=jnp.float32)
        sums = product if sums is None else sums + product

    halves = [sums[:, 128 * j : 128 * (j + 1)] for j in range(chans // 128)]

    @pl.when(dt == 0)
    def _():
        for j, half in enumerate(halves):
            total[j] = half

    @pl.when(dt > 0)
    def _():
        for j, half in enumerate(halves):
            total[j] += half

    @pl.when(dt == 2)
    def _():
        pieces = []
        for d in range(skip_a_ref.shape[1] // 16):
            pieces += [skip_a_ref[0, 16 * d : 16 * d + 16], skip_b_ref[0, 16 * d : 16 * d + 16]]
        skip = jnp.concatenate(pieces, axis=0)
        shortcut = jnp.dot(features_ref[...], skip, preferred_element_type=jnp.float32) + bias_ref[...]
        for t in range(2):
            for y in range(6):
                conv = [total[j, pl.ds(128 * t + y, 16, stride=8), :] for j in range(chans // 128)]
                conv = jnp.concatenate(conv, axis=1)
                at = (6 * t + y) * 16
                out_ref[pl.ds(at, 16), :] = (conv + shortcut[at : at + 16]).astype(jnp.bfloat16)


def whole(*_):
    return pl.BlockSpec(memory_space=VMEM)


def per_device(
    features,
    gn1_gain,
    gn1_bias,
    conv1_weight,
    conv1_bias,
    skip_weight,
    gn2_gain,
    gn2_bias,
    conv2_weight,
    conv2_bias,
):
    frames, rows, cols, chans_in = features.shape
    chans_out = conv1_weight.shape[2]
    ntm, nrow, ncol = (lax.axis_size(a) for a in ("tm", "row", "col"))
    tm, row, col = (lax.axis_index(a) for a in ("tm", "row", "col"))
    place = jnp.stack([row, col, tm]).astype(jnp.int32)
    positions = frames * rows * cols
    plane = nrow * ncol
    flat_features = features.reshape(positions, chans_in)
    tile = jax.ShapeDtypeStruct((8, 128), jnp.float32)

    first_weight = lax.all_gather(conv1_weight, ("row", "col"), axis=1, tiled=True)
    share = conv2_weight.shape[1]
    halves = skip_weight.reshape(2, share, chans_out)
    later = lax.all_gather(
        jnp.concatenate([conv2_weight, halves], axis=0), ("row", "col"), axis=1, tiled=True
    )

    def shared(stats, count):
        stats = lax.all_to_all(stats, ("row", "col"), 0, 0, tiled=True)
        stats = pl.pallas_call(
            functools.partial(merge_kernel, count),
            out_shape=jax.ShapeDtypeStruct((ntm, *tile.shape), tile.dtype),
            in_specs=[whole()],
            out_specs=whole(),
        )(stats)
        return lax.all_to_all(stats, "tm", 0, 0, tiled=True)

    stats = pl.pallas_call(
        stats_kernel,
        out_shape=jax.ShapeDtypeStruct((plane, *tile.shape), tile.dtype),
        in_specs=[whole()],
        out_specs=whole(),
    )(flat_features)
    parts = shared(stats, float(positions))

    back_one = moved(features, "tm", 1)
    back_two = moved(features, "tm", 2)
    first_twice = jnp.concatenate([features[:1], features[:1]], axis=0)
    back_one = jnp.where(tm == 0, first_twice, back_one)
    earliest = jnp.concatenate([back_one[:1], back_one[:1]], axis=0)
    back_two = jnp.where(tm <= 1, earliest, back_two)
    volume = jnp.concatenate([back_two, back_one, features], axis=0)

    above = moved(volume[:, -2:], "row", 1)
    below = moved(volume[:, :2], "row", -1)
    edge = [jnp.where(col == 0, part[:, :, -2:], part[:, :, :2]) for part in (above, volume, below)]
    edge[0] = jnp.where(row == 0, edge[1][:, :1], edge[0])
    edge[2] = jnp.where(row == nrow - 1, edge[1][:, -1:], edge[2])
    border = jnp.concatenate(edge, axis=1).transpose(0, 2, 1, 3)
    border = jnp.pad(border, ((0, 0), (0, 0), (0, 16 - border.shape[2]), (0, 0)))
    border = swapped(border, "col")

    copies = pl.pallas_call(
        functools.partial(hidden1_kernel, float(positions * plane), ntm),
        out_shape=jax.ShapeDtypeStruct((6, 960, chans_in), jnp.bfloat16),
        in_specs=[pl.BlockSpec(memory_space=SMEM)] + [whole()] * 7,
        out_specs=whole(),
        scratch_shapes=[VMEM((chans_in // 128, 160, 128), jnp.float32), VMEM((32, chans_in), jnp.float32)],
        compiler_params=pltpu.CompilerParams(vmem_limit_bytes=24 * MIB),
    )(place, parts, gn1_gain[None], gn1_bias[None], volume, above, below, border)

    middle, stats = pl.pallas_call(
        functools.partial(conv1_kernel, float(positions)),
        grid=(3, 3),
        out_shape=(
            jax.ShapeDtypeStruct((576, chans_out), jnp.float32),
            jax.ShapeDtypeStruct((plane, *tile.shape), tile.dtype),
        ),
        in_specs=[
            pl.BlockSpec((2, 960, chans_in), lambda dy, dt: (dy, 0, 0)),
            pl.BlockSpec((3, chans_in, chans_out), lambda dy, dt: (3 * dt + dy, 0, 0)),
            pl.BlockSpec((1, chans_out), lambda dy, dt: (0, 0)),
        ],
        out_specs=(
            pl.BlockSpec((576, chans_out), lambda dy, dt: (0, 0)),
            pl.BlockSpec((plane, 8, 128), lambda dy, dt: (0, 0, 0)),
        ),
        compiler_params=pltpu.CompilerParams(vmem_limit_bytes=32 * MIB),
    )(copies, first_weight, conv1_bias[None])

    parts = shared(stats, float(positions))

    out = pl.pallas_call(
        functools.partial(conv2_kernel, float(positions * plane), ntm),
        grid=(3,),
        out_shape=jax.ShapeDtypeStruct((positions, chans_out), jnp.bfloat16),
        in_specs=[
            pl.BlockSpec(memory_space=SMEM),
            pl.BlockSpec((ntm, 8, 128), lambda dt: (0, 0, 0)),
            pl.BlockSpec((1, chans_out), lambda dt: (0, 0)),
            pl.BlockSpec((1, chans_out), lambda dt: (0, 0)),
            pl.BlockSpec((1, chans_out), lambda dt: (0, 0)),
            pl.BlockSpec((576, chans_out), lambda dt: (0, 0)),
            pl.BlockSpec((positions, chans_in), lambda dt: (0, 0)),
            pl.BlockSpec((9, chans_out, chans_out), lambda dt: (dt, 0, 0)),
            pl.BlockSpec((1, chans_out, chans_out), lambda dt: (27, 0, 0)),
            pl.BlockSpec((1, chans_out, chans_out), lambda dt: (28, 0, 0)),
        ],
        out_specs=pl.BlockSpec((positions, chans_out), lambda dt: (0, 0)),
        scratch_shapes=[
            VMEM((6, 576, chans_out), jnp.bfloat16),
            VMEM((chans_out // 128, 256, 128), jnp.float32),
        ],
        compiler_params=pltpu.CompilerParams(vmem_limit_bytes=24 * MIB),
    )(place, parts, gn2_gain[None], gn2_bias[None], conv2_bias[None], middle, flat_features, later, later, later)
    return out.reshape(frames, rows, cols, chans_out)


def solution(mesh):
    in_specs = (
        P("tm", "row", "col", None),
        P(),
        P(),
        P(None, ("row", "col"), None),
        P(),
        P(None, ("row", "col"), None),
        P(),
        P(),
        P(None, ("row", "col"), None),
        P(),
    )
    out_specs = P("tm", "row", "col", None)
    return jax.shard_map(
        per_device, mesh=mesh, in_specs=in_specs, out_specs=out_specs, check_vma=False
    )
```

```python
import functools

import jax
import jax.numpy as jnp
from jax import lax
from jax.experimental import pallas as pl
from jax.experimental.pallas import tpu as pltpu
from jax.sharding import Mesh
from jax.sharding import PartitionSpec as P

GROUPS = 32
TM = ("x", "z")
MIB = 1024 * 1024
VMEM = pltpu.VMEM
SMEM = pltpu.SMEM
HBM = pltpu.HBM


def moved(block, axis, distance):
    size = lax.axis_size(axis)
    route = [(i, i + distance) for i in range(size) if 0 <= i + distance < size]
    return lax.ppermute(block, axis, route)


def swapped(block, axis):
    return lax.ppermute(block, axis, [(0, 1), (1, 0)])


def as_rows(row):
    return jnp.concatenate([row[:, 128 * j : 128 * (j + 1)] for j in range(row.shape[1] // 128)], axis=0)


def as_row(rows):
    return jnp.concatenate([rows[j : j + 1] for j in range(rows.shape[0])], axis=1)


def packed(mean, squares):
    half = 4
    mean, squares = as_rows(mean), as_rows(squares)
    if mean.shape[0] < half:
        blank = jnp.zeros((half - mean.shape[0], 128), jnp.float32)
        mean = jnp.concatenate([mean, blank], axis=0)
        squares = jnp.concatenate([squares, blank], axis=0)
    return jnp.concatenate([mean, squares], axis=0)


def merged(parts_ref, count):
    parts = parts_ref[...]
    total = jnp.sum(parts, axis=0)
    mean = total / parts.shape[0]
    off = parts - mean[None]
    between = jnp.sum(off * off, axis=0)
    return jnp.concatenate([mean[:4], total[4:] + count * between[:4]], axis=0)


def group_average(rows, size):
    lane = lax.broadcasted_iota(jnp.int32, rows.shape, 1)
    step = 1
    while step < size:
        up, down = pltpu.roll(rows, 128 - step, 1), pltpu.roll(rows, step, 1)
        rows = rows + jnp.where((lane & step) == 0, up, down)
        step *= 2
    return rows / size


def group_moments(tile, count, size, chans):
    mean, squares = tile[:4], tile[4:]
    centre = group_average(mean, size)
    off = mean - centre
    variance = group_average(squares / count + off * off, size)
    scale = lax.rsqrt(variance + 1e-06)
    k = chans // 128
    return as_row(centre[:k]), as_row(scale[:k])


def silu_of(values, mean, scale, gain, shift):
    return jax.nn.silu((values - mean) * scale * gain + shift)


def channel_stats(values, keep, count):
    if keep is not None:
        mean = jnp.sum(jnp.where(keep, values, 0.0), axis=0, keepdims=True) / count
        off = jnp.where(keep, values - mean, 0.0)
    else:
        mean = jnp.sum(values, axis=0, keepdims=True) / count
        off = values - mean
    return packed(mean, jnp.sum(off * off, axis=0, keepdims=True))


def stats_kernel(x_ref, out_ref):
    values = x_ref[...].astype(jnp.float32)
    tile = channel_stats(values, None, float(values.shape[0]))
    out_ref[...] = jnp.broadcast_to(tile[None], out_ref.shape)


def merge_kernel(count, parts_ref, out_ref):
    out_ref[...] = jnp.broadcast_to(merged(parts_ref, count)[None], out_ref.shape)


def border_kernel(place_ref, centre_ref, above_ref, below_ref, out_ref, plain):
    row, col = place_ref[0], place_ref[1]
    pieces = plain.shape[0]

    def put(y, block):
        block = block.astype(jnp.float32)
        for j in range(pieces):
            plain[j, 16 * y : 16 * y + 16, :] = block[:, 128 * j : 128 * (j + 1)]

    plain[...] = jnp.zeros_like(plain)

    def frame(t, _):
        for y in range(2):
            put(y, jnp.where(row == 0, centre_ref[t, 0], above_ref[t, y]))
            put(y + 8, jnp.where(row == 7, centre_ref[t, 5], below_ref[t, y]))
        for y in range(6):
            put(y + 2, centre_ref[t, y])

        def column(x):
            return jnp.concatenate([plain[j, pl.ds(x, 16, stride=16), :] for j in range(pieces)], axis=1)

        for x in range(2):
            out_ref[t, x] = jnp.where(col == 0, column(14 + x), column(x)).astype(jnp.bfloat16)
        return 0

    lax.fori_loop(0, 6, frame, 0)


def hidden1_kernel(
    count, peers, place_ref, parts_ref, gain_ref, shift_ref, centre_ref, above_ref, below_ref, border_ref, out_ref, plain, side
):
    chans = centre_ref.shape[-1]
    tile = merged(parts_ref, count)
    mean, scale = group_moments(tile, count * peers, chans // GROUPS, chans)
    gain, shift = gain_ref[...], shift_ref[...]
    row, col = place_ref[0], place_ref[1]

    def normed(block):
        return silu_of(block.astype(jnp.float32), mean, scale, gain, shift)

    def put(y, block):
        for j in range(chans // 128):
            plain[j, 16 * y : 16 * y + 16, :] = block[:, 128 * j : 128 * (j + 1)]

    def frame(t, _):
        own = [normed(centre_ref[t, y]) for y in range(6)]
        for y in range(2):
            put(y, jnp.where(row == 0, own[0], normed(above_ref[t, y])))
            put(y + 8, jnp.where(row == 7, own[5], normed(below_ref[t, y])))
        for y in range(6):
            put(y + 2, own[y])
        for x in range(2):
            side[pl.ds(16 * x, 16), :] = normed(border_ref[t, x])
        for dy in range(3):

            def column(x):
                pieces = [plain[j, pl.ds(16 * dy + x, 8, stride=16), :] for j in range(chans // 128)]
                return jnp.concatenate(pieces, axis=1)

            inner = [column(x) for x in range(16)]
            outer = [side[pl.ds(16 * x + dy, 8), :] for x in range(2)]
            left = [jnp.where(col == 0, inner[0], o) for o in outer]
            right = [jnp.where(col == 0, o, inner[15]) for o in outer]
            columns = left + inner + right
            base = pl.multiple_of(t * 160, 16)
            for p in range(2):
                for i in range(10 - p):
                    pair = jnp.concatenate([columns[2 * i + p], columns[2 * i + p + 1]], axis=0)
                    out_ref[2 * dy + p, pl.ds(base + 16 * i, 16), :] = pair.astype(jnp.bfloat16)
            out_ref[2 * dy + 1, pl.ds(base + 144, 16), :] = jnp.zeros((16, chans), jnp.bfloat16)
        return 0

    lax.fori_loop(0, 6, frame, 0)


def conv1_kernel(count, bias_ref, copies_ref, gathered_ref, middle_ref, stats_ref, copies, weights, arrived):
    layouts = [pltpu.make_async_copy(copies_ref.at[i], copies.at[i], arrived.at[i]) for i in range(6)]
    fetches = [
        pltpu.make_async_copy(gathered_ref.at[3 * i : 3 * i + 3], weights.at[3 * i : 3 * i + 3], arrived.at[6 + i])
        for i in range(9)
    ]
    for dy in range(3):
        for copy in [*layouts[2 * dy : 2 * dy + 2], *fetches[dy::3]]:
            copy.start()
    middle_ref[...] = jnp.broadcast_to(bias_ref[...], middle_ref.shape)
    depth = 3 * weights.shape[1]
    for dy in range(3):
        for copy in layouts[2 * dy : 2 * dy + 2]:
            copy.wait()
        for dt in range(3):
            fetches[3 * dt + dy].wait()
            weight = weights[9 * dt + 3 * dy : 9 * dt + 3 * dy + 3].reshape(depth, weights.shape[2])
            for half in range(2):

                def window(dx, dy=dy, first=dt + 2 * half):
                    starts = [(first + t) * 160 + (dx // 2) * 16 for t in range(2)]
                    return jnp.concatenate([copies[2 * dy + dx % 2, at : at + 144, :] for at in starts], axis=0)

                lhs = jnp.concatenate([window(dx) for dx in range(3)], axis=1)
                product = jnp.dot(lhs, weight, preferred_element_type=jnp.float32)
                middle_ref[288 * half : 288 * half + 288, :] += product

    values = middle_ref[288:, :]
    place = lax.broadcasted_iota(jnp.int32, values.shape, 0)
    y, x = place % 8, (place // 8) % 18
    keep = (y >= 1) & (y <= 6) & (x >= 1) & (x <= 16)
    tile = channel_stats(values, keep, count)
    stats_ref[...] = jnp.broadcast_to(tile[None], stats_ref.shape)


def hidden2_kernel(count, peers, place_ref, parts_ref, gain_ref, shift_ref, middle_ref, copies):
    row, col, tm = place_ref[0], place_ref[1], place_ref[2]
    chans = middle_ref.shape[1]
    tile = merged(parts_ref, count)
    mean, scale = group_moments(tile, count * peers, chans // GROUPS, chans)
    gain, shift = gain_ref[...], shift_ref[...]
    y = lax.broadcasted_iota(jnp.int32, (8, chans), 0)
    for t in range(4):
        source = jnp.where(tm == 0, 2, t) if t < 2 else t
        block = middle_ref[pl.ds(pl.multiple_of(source * 144, 16), 144), :]
        block = silu_of(block, mean, scale, gain, shift)
        columns = [block[8 * x : 8 * x + 8] for x in range(18)]
        columns[0] = jnp.where(col == 0, columns[1], columns[0])
        columns[17] = jnp.where(col == 1, columns[16], columns[17])
        for x in range(18):
            column = columns[x]
            column = jnp.where((y == 0) & (row == 0), pltpu.roll(column, 7, 0), column)
            columns[x] = jnp.where((y == 7) & (row == 7), pltpu.roll(column, 1, 0), column)
        for dy in range(3):
            rolled = columns if dy == 0 else [pltpu.roll(c, 8 - dy, 0) for c in columns]
            for p in range(2):
                for i in range(9 - p):
                    pair = jnp.concatenate([rolled[2 * i + p], rolled[2 * i + p + 1]], axis=0)
                    copies[2 * dy + p, 144 * t + 16 * i : 144 * t + 16 * i + 16, :] = pair.astype(jnp.bfloat16)


def conv2_kernel(copies, bias_ref, features_ref, weight_ref, out_ref, total):
    chans = weight_ref.shape[3]

    def tap(k):
        return weight_ref[k // 2, :, 16 * (k % 2) : 16 * (k % 2) + 16, :].reshape(chans, chans)

    rows = [weight_ref[(27 + h) // 2, d, 16 * ((27 + h) % 2) : 16 * ((27 + h) % 2) + 16, :] for d in range(chans // 16) for h in range(2)]
    skip = jnp.concatenate(rows, axis=0)
    shortcut = jnp.dot(features_ref[...], skip, preferred_element_type=jnp.float32) + bias_ref[...]
    for dt in range(3):
        for dy in range(3):
            weight = jnp.concatenate([tap(9 * dt + 3 * dy + dx) for dx in range(3)], axis=0)
            for t in range(2):

                def window(dx, dy=dy, first=dt + t):
                    start = first * 144 + (dx // 2) * 16
                    return copies[2 * dy + dx % 2, start : start + 128, :]

                lhs = jnp.concatenate([window(dx) for dx in range(3)], axis=1)
                product = jnp.dot(lhs, weight, preferred_element_type=jnp.float32)
                for j in range(chans // 128):
                    part = product[:, 128 * j : 128 * (j + 1)]
                    if dt == 0 and dy == 0:
                        total[j, 128 * t : 128 * t + 128, :] = part
                    else:
                        total[j, 128 * t : 128 * t + 128, :] += part

    for t in range(2):
        for y in range(6):
            conv = [total[j, pl.ds(128 * t + y, 16, stride=8), :] for j in range(chans // 128)]
            at = (6 * t + y) * 16
            out_ref[at : at + 16, :] = (jnp.concatenate(conv, axis=1) + shortcut[at : at + 16]).astype(jnp.bfloat16)


def whole(*_):
    return pl.BlockSpec(memory_space=VMEM)


def per_device(
    features,
    gn1_gain,
    gn1_bias,
    conv1_weight,
    conv1_bias,
    skip_weight,
    gn2_gain,
    gn2_bias,
    conv2_weight,
    conv2_bias,
):
    frames, rows, cols, chans_in = features.shape
    chans_out = conv1_weight.shape[2]
    ntm, nrow, ncol = (lax.axis_size(a) for a in (TM, "row", "col"))
    tm, row, col = (lax.axis_index(a) for a in (TM, "row", "col"))
    place = jnp.stack([row, col, tm]).astype(jnp.int32)
    positions = frames * rows * cols
    plane = nrow * ncol
    flat_features = features.reshape(positions, chans_in)
    tile = jax.ShapeDtypeStruct((8, 128), jnp.float32)

    share = conv2_weight.shape[1]
    spare = jnp.zeros((3, share, chans_out), jnp.bfloat16)
    later = jnp.concatenate([conv2_weight, skip_weight.reshape(2, share, chans_out), spare], axis=0)
    later = later.reshape(16, 2 * share, chans_out)
    later = lax.dynamic_slice_in_dim(later, 4 * lax.axis_index("x"), 4, axis=0)
    taps = conv1_weight.shape[0]
    first = lax.all_gather(
        jnp.concatenate([conv1_weight, later], axis=0), ("row", "col"), axis=1, tiled=True
    )
    def shared(stats, count, beside=()):
        stats = lax.all_to_all(stats, ("row", "col"), 0, 0, tiled=True)
        if beside:
            stats, beside = lax.optimization_barrier((stats, beside))
        stats = pl.pallas_call(
            functools.partial(merge_kernel, count),
            out_shape=jax.ShapeDtypeStruct((ntm, *tile.shape), tile.dtype),
            in_specs=[whole()],
            out_specs=whole(),
        )(stats)
        return lax.all_to_all(stats, TM, 0, 0, tiled=True), beside

    stats = pl.pallas_call(
        stats_kernel,
        out_shape=jax.ShapeDtypeStruct((plane, *tile.shape), tile.dtype),
        in_specs=[whole()],
        out_specs=whole(),
    )(flat_features)
    back_one = moved(features, TM, 1)
    back_two = moved(features, TM, 2)
    first_twice = jnp.concatenate([features[:1], features[:1]], axis=0)
    back_one = jnp.where(tm == 0, first_twice, back_one)
    earliest = jnp.concatenate([back_one[:1], back_one[:1]], axis=0)
    back_two = jnp.where(tm <= 1, earliest, back_two)
    volume = jnp.concatenate([back_two, back_one, features], axis=0)

    parts, (last, leading) = shared(stats, float(positions), (volume[:, -2:], volume[:, :2]))
    above = moved(last, "row", 1)
    below = moved(leading, "row", -1)

    border = pl.pallas_call(
        border_kernel,
        out_shape=jax.ShapeDtypeStruct((volume.shape[0], 2, 16, chans_in), jnp.bfloat16),
        in_specs=[pl.BlockSpec(memory_space=SMEM)] + [whole()] * 3,
        out_specs=whole(),
        scratch_shapes=[VMEM((chans_in // 128, 256, 128), jnp.float32)],
        compiler_params=pltpu.CompilerParams(vmem_limit_bytes=16 * MIB),
    )(place, volume, above, below)
    border = swapped(border, "col")

    copies = pl.pallas_call(
        functools.partial(hidden1_kernel, float(positions * plane), ntm),
        out_shape=jax.ShapeDtypeStruct((6, 960, chans_in), jnp.bfloat16),
        in_specs=[pl.BlockSpec(memory_space=SMEM)] + [whole()] * 7,
        out_specs=whole(),
        scratch_shapes=[VMEM((chans_in // 128, 160, 128), jnp.float32), VMEM((32, chans_in), jnp.float32)],
        compiler_params=pltpu.CompilerParams(vmem_limit_bytes=24 * MIB),
    )(place, parts, gn1_gain[None], gn1_bias[None], volume, above, below, border)

    copies, first = lax.optimization_barrier((copies, first))
    half = lax.dynamic_slice_in_dim(first, taps + 2 * col, 2, axis=0)
    second = lax.all_gather(half, ("x", "col"), axis=0, tiled=True)
    second = second.reshape(16, plane, 2 * share, chans_out)

    middle, stats = pl.pallas_call(
        functools.partial(conv1_kernel, float(positions)),
        out_shape=(
            jax.ShapeDtypeStruct((576, chans_out), jnp.float32),
            jax.ShapeDtypeStruct((plane, *tile.shape), tile.dtype),
        ),
        in_specs=[whole()] + [pl.BlockSpec(memory_space=HBM)] * 2,
        out_specs=(whole(), whole()),
        scratch_shapes=[
            VMEM(copies.shape, jnp.bfloat16),
            VMEM((taps, chans_in, chans_out), jnp.bfloat16),
            pltpu.SemaphoreType.DMA((15,)),
        ],
        compiler_params=pltpu.CompilerParams(vmem_limit_bytes=60 * MIB),
    )(conv1_bias[None], copies, first)

    parts, _ = shared(stats, float(positions))

    copies = pl.pallas_call(
        functools.partial(hidden2_kernel, float(positions * plane), ntm),
        out_shape=jax.ShapeDtypeStruct((6, 576, chans_out), jnp.bfloat16),
        in_specs=[pl.BlockSpec(memory_space=SMEM)] + [whole()] * 4,
        out_specs=whole(),
        compiler_params=pltpu.CompilerParams(vmem_limit_bytes=16 * MIB),
    )(place, parts, gn2_gain[None], gn2_bias[None], middle)

    copies, second = lax.optimization_barrier((copies, second))
    out = pl.pallas_call(
        conv2_kernel,
        out_shape=jax.ShapeDtypeStruct((positions, chans_out), jnp.bfloat16),
        in_specs=[whole()] * 4,
        out_specs=whole(),
        scratch_shapes=[VMEM((chans_out // 128, 256, 128), jnp.float32)],
        compiler_params=pltpu.CompilerParams(vmem_limit_bytes=24 * MIB),
    )(copies, conv2_bias[None], flat_features, second)
    return out.reshape(frames, rows, cols, chans_out)


def solution(mesh):
    mesh = Mesh(mesh.devices.reshape(4, -1, *mesh.devices.shape[1:]), (*TM, "row", "col"))
    in_specs = (
        P(TM, "row", "col", None),
        P(),
        P(),
        P(None, ("row", "col"), None),
        P(),
        P(None, ("row", "col"), None),
        P(),
        P(),
        P(None, ("row", "col"), None),
        P(),
    )
    out_specs = P(TM, "row", "col", None)
    return jax.shard_map(
        per_device, mesh=mesh, in_specs=in_specs, out_specs=out_specs, check_vma=False
    )
```

```python
import functools

import jax
import jax.numpy as jnp
from jax import lax
from jax.experimental import pallas as pl
from jax.experimental.pallas import tpu as pltpu
from jax.sharding import Mesh
from jax.sharding import PartitionSpec as P

GROUPS = 32
TM = ("x", "z")
MIB = 1024 * 1024
VMEM = pltpu.VMEM
SMEM = pltpu.SMEM
HBM = pltpu.HBM


def moved(block, axis, distance):
    size = lax.axis_size(axis)
    route = [(i, i + distance) for i in range(size) if 0 <= i + distance < size]
    return lax.ppermute(block, axis, route)


def swapped(block, axis):
    return lax.ppermute(block, axis, [(0, 1), (1, 0)])


def as_rows(row):
    return jnp.concatenate([row[:, 128 * j : 128 * (j + 1)] for j in range(row.shape[1] // 128)], axis=0)


def as_row(rows):
    return jnp.concatenate([rows[j : j + 1] for j in range(rows.shape[0])], axis=1)


def packed(mean, squares):
    half = 4
    mean, squares = as_rows(mean), as_rows(squares)
    if mean.shape[0] < half:
        blank = jnp.zeros((half - mean.shape[0], 128), jnp.float32)
        mean = jnp.concatenate([mean, blank], axis=0)
        squares = jnp.concatenate([squares, blank], axis=0)
    return jnp.concatenate([mean, squares], axis=0)


def merged(parts_ref, count):
    parts = parts_ref[...]
    total = jnp.sum(parts, axis=0)
    mean = total / parts.shape[0]
    off = parts - mean[None]
    between = jnp.sum(off * off, axis=0)
    return jnp.concatenate([mean[:4], total[4:] + count * between[:4]], axis=0)


def group_average(rows, size):
    lane = lax.broadcasted_iota(jnp.int32, rows.shape, 1)
    step = 1
    while step < size:
        up, down = pltpu.roll(rows, 128 - step, 1), pltpu.roll(rows, step, 1)
        rows = rows + jnp.where((lane & step) == 0, up, down)
        step *= 2
    return rows / size


def group_moments(tile, count, size, chans):
    mean, squares = tile[:4], tile[4:]
    centre = group_average(mean, size)
    off = mean - centre
    variance = group_average(squares / count + off * off, size)
    scale = lax.rsqrt(variance + 1e-06)
    k = chans // 128
    return as_row(centre[:k]), as_row(scale[:k])


def silu_of(values, mean, scale, gain, shift):
    return jax.nn.silu((values - mean) * scale * gain + shift)


def channel_stats(values, keep, count):
    if keep is not None:
        mean = jnp.sum(jnp.where(keep, values, 0.0), axis=0, keepdims=True) / count
        off = jnp.where(keep, values - mean, 0.0)
    else:
        mean = jnp.sum(values, axis=0, keepdims=True) / count
        off = values - mean
    return packed(mean, jnp.sum(off * off, axis=0, keepdims=True))


def stats_kernel(x_ref, out_ref):
    values = x_ref[...].astype(jnp.float32)
    tile = channel_stats(values, None, float(values.shape[0]))
    out_ref[...] = jnp.broadcast_to(tile[None], out_ref.shape)


def merge_kernel(count, parts_ref, out_ref):
    out_ref[...] = jnp.broadcast_to(merged(parts_ref, count)[None], out_ref.shape)


def border_kernel(place_ref, centre_ref, above_ref, below_ref, out_ref, plain):
    row, col = place_ref[0], place_ref[1]
    pieces = plain.shape[0]

    def put(y, block):
        block = block.astype(jnp.float32)
        for j in range(pieces):
            plain[j, 16 * y : 16 * y + 16, :] = block[:, 128 * j : 128 * (j + 1)]

    plain[...] = jnp.zeros_like(plain)

    def frame(t, _):
        for y in range(2):
            put(y, jnp.where(row == 0, centre_ref[t, 0], above_ref[t, y]))
            put(y + 8, jnp.where(row == 7, centre_ref[t, 5], below_ref[t, y]))
        for y in range(6):
            put(y + 2, centre_ref[t, y])

        def column(x):
            return jnp.concatenate([plain[j, pl.ds(x, 16, stride=16), :] for j in range(pieces)], axis=1)

        for x in range(2):
            out_ref[t, x] = jnp.where(col == 0, column(14 + x), column(x)).astype(jnp.bfloat16)
        return 0

    lax.fori_loop(0, 4, frame, 0)


def hidden1_kernel(
    count, peers, place_ref, parts_ref, gain_ref, shift_ref, centre_ref, above_ref, below_ref, border_ref, out_ref, plain, side
):
    chans = centre_ref.shape[-1]
    tile = merged(parts_ref, count)
    mean, scale = group_moments(tile, count * peers, chans // GROUPS, chans)
    gain, shift = gain_ref[...], shift_ref[...]
    row, col = place_ref[0], place_ref[1]

    def normed(block):
        return silu_of(block.astype(jnp.float32), mean, scale, gain, shift)

    def put(y, block):
        for j in range(chans // 128):
            plain[j, 16 * y : 16 * y + 16, :] = block[:, 128 * j : 128 * (j + 1)]

    def frame(t, _):
        own = [normed(centre_ref[t, y]) for y in range(6)]
        for y in range(2):
            put(y, jnp.where(row == 0, own[0], normed(above_ref[t, y])))
            put(y + 8, jnp.where(row == 7, own[5], normed(below_ref[t, y])))
        for y in range(6):
            put(y + 2, own[y])
        for x in range(2):
            side[pl.ds(16 * x, 16), :] = normed(border_ref[t, x])
        for dy in range(3):

            def column(x):
                pieces = [plain[j, pl.ds(16 * dy + x, 8, stride=16), :] for j in range(chans // 128)]
                return jnp.concatenate(pieces, axis=1)

            inner = [column(x) for x in range(16)]
            outer = [side[pl.ds(16 * x + dy, 8), :] for x in range(2)]
            left = [jnp.where(col == 0, inner[0], o) for o in outer]
            right = [jnp.where(col == 0, o, inner[15]) for o in outer]
            columns = left + inner + right
            base = pl.multiple_of(t * 160, 16)
            for p in range(2):
                for i in range(10 - p):
                    pair = jnp.concatenate([columns[2 * i + p], columns[2 * i + p + 1]], axis=0)
                    out_ref[2 * dy + p, pl.ds(base + 16 * i, 16), :] = pair.astype(jnp.bfloat16)
            out_ref[2 * dy + 1, pl.ds(base + 144, 16), :] = jnp.zeros((16, chans), jnp.bfloat16)
        return 0

    lax.fori_loop(0, 4, frame, 0)


def conv1_kernel(count, bias_ref, copies_ref, gathered_ref, middle_ref, stats_ref, copies, weights, arrived):
    layouts = [pltpu.make_async_copy(copies_ref.at[i], copies.at[i], arrived.at[i]) for i in range(6)]
    fetches = [
        pltpu.make_async_copy(gathered_ref.at[3 * i : 3 * i + 3], weights.at[3 * i : 3 * i + 3], arrived.at[6 + i])
        for i in range(9)
    ]
    for dy in range(3):
        for copy in [*layouts[2 * dy : 2 * dy + 2], *fetches[dy::3]]:
            copy.start()
    middle_ref[...] = jnp.broadcast_to(bias_ref[...], middle_ref.shape)
    depth = 3 * weights.shape[1]
    for dy in range(3):
        for copy in layouts[2 * dy : 2 * dy + 2]:
            copy.wait()
        for dt in range(3):
            fetches[3 * dt + dy].wait()
            weight = weights[9 * dt + 3 * dy : 9 * dt + 3 * dy + 3].reshape(depth, weights.shape[2])

            def window(dx, dy=dy, dt=dt):
                starts = [(dt + t) * 160 + (dx // 2) * 16 for t in range(2)]
                return jnp.concatenate([copies[2 * dy + dx % 2, at : at + 144, :] for at in starts], axis=0)

            lhs = jnp.concatenate([window(dx) for dx in range(3)], axis=1)
            middle_ref[...] += jnp.dot(lhs, weight, preferred_element_type=jnp.float32)

    values = middle_ref[...]
    place = lax.broadcasted_iota(jnp.int32, values.shape, 0)
    y, x = place % 8, (place // 8) % 18
    keep = (y >= 1) & (y <= 6) & (x >= 1) & (x <= 16)
    tile = channel_stats(values, keep, count)
    stats_ref[...] = jnp.broadcast_to(tile[None], stats_ref.shape)


def hidden2_kernel(count, peers, place_ref, parts_ref, gain_ref, shift_ref, earlier_ref, middle_ref, copies):
    row, col, tm = place_ref[0], place_ref[1], place_ref[2]
    chans = middle_ref.shape[1]
    tile = merged(parts_ref, count)
    mean, scale = group_moments(tile, count * peers, chans // GROUPS, chans)
    gain, shift = gain_ref[...], shift_ref[...]
    y = lax.broadcasted_iota(jnp.int32, (8, chans), 0)
    for t in range(4):
        if t < 2:
            block = jnp.where(tm == 0, middle_ref[:144, :], earlier_ref[144 * t : 144 * t + 144, :])
        else:
            block = middle_ref[144 * (t - 2) : 144 * (t - 1), :]
        block = silu_of(block, mean, scale, gain, shift)
        columns = [block[8 * x : 8 * x + 8] for x in range(18)]
        columns[0] = jnp.where(col == 0, columns[1], columns[0])
        columns[17] = jnp.where(col == 1, columns[16], columns[17])
        for x in range(18):
            column = columns[x]
            column = jnp.where((y == 0) & (row == 0), pltpu.roll(column, 7, 0), column)
            columns[x] = jnp.where((y == 7) & (row == 7), pltpu.roll(column, 1, 0), column)
        for dy in range(3):
            rolled = columns if dy == 0 else [pltpu.roll(c, 8 - dy, 0) for c in columns]
            for p in range(2):
                for i in range(9 - p):
                    pair = jnp.concatenate([rolled[2 * i + p], rolled[2 * i + p + 1]], axis=0)
                    copies[2 * dy + p, 144 * t + 16 * i : 144 * t + 16 * i + 16, :] = pair.astype(jnp.bfloat16)


def conv2_kernel(copies, bias_ref, features_ref, weight_ref, out_ref, total):
    chans = weight_ref.shape[2]
    rows = [weight_ref[27 + h, 16 * d : 16 * d + 16, :] for d in range(chans // 16) for h in range(2)]
    skip = jnp.concatenate(rows, axis=0)
    shortcut = jnp.dot(features_ref[...], skip, preferred_element_type=jnp.float32) + bias_ref[...]
    for dt in range(3):
        for dy in range(3):
            weight = weight_ref[9 * dt + 3 * dy : 9 * dt + 3 * dy + 3].reshape(3 * chans, chans)
            for t in range(2):

                def window(dx, dy=dy, first=dt + t):
                    start = first * 144 + (dx // 2) * 16
                    return copies[2 * dy + dx % 2, start : start + 128, :]

                lhs = jnp.concatenate([window(dx) for dx in range(3)], axis=1)
                product = jnp.dot(lhs, weight, preferred_element_type=jnp.float32)
                for j in range(chans // 128):
                    part = product[:, 128 * j : 128 * (j + 1)]
                    if dt == 0 and dy == 0:
                        total[j, 128 * t : 128 * t + 128, :] = part
                    else:
                        total[j, 128 * t : 128 * t + 128, :] += part

    for t in range(2):
        for y in range(6):
            conv = [total[j, pl.ds(128 * t + y, 16, stride=8), :] for j in range(chans // 128)]
            at = (6 * t + y) * 16
            out_ref[at : at + 16, :] = (jnp.concatenate(conv, axis=1) + shortcut[at : at + 16]).astype(jnp.bfloat16)


def whole(*_):
    return pl.BlockSpec(memory_space=VMEM)


def per_device(
    features,
    gn1_gain,
    gn1_bias,
    conv1_weight,
    conv1_bias,
    skip_weight,
    gn2_gain,
    gn2_bias,
    conv2_weight,
    conv2_bias,
):
    frames, rows, cols, chans_in = features.shape
    chans_out = conv1_weight.shape[2]
    ntm, nrow, ncol = (lax.axis_size(a) for a in (TM, "row", "col"))
    tm, row, col = (lax.axis_index(a) for a in (TM, "row", "col"))
    place = jnp.stack([row, col, tm]).astype(jnp.int32)
    positions = frames * rows * cols
    plane = nrow * ncol
    flat_features = features.reshape(positions, chans_in)
    tile = jax.ShapeDtypeStruct((8, 128), jnp.float32)

    first = lax.all_gather(conv1_weight, ("row", "col"), axis=1, tiled=True)
    share = conv2_weight.shape[1]
    halves = skip_weight.reshape(2, share, chans_out)
    second = lax.all_gather(jnp.concatenate([conv2_weight, halves], axis=0), ("row", "col"), axis=1, tiled=True)

    def shared(stats, count, beside=()):
        stats = lax.all_to_all(stats, ("row", "col"), 0, 0, tiled=True)
        if beside:
            stats, beside = lax.optimization_barrier((stats, beside))
        stats = pl.pallas_call(
            functools.partial(merge_kernel, count),
            out_shape=jax.ShapeDtypeStruct((ntm, *tile.shape), tile.dtype),
            in_specs=[whole()],
            out_specs=whole(),
        )(stats)
        return lax.all_to_all(stats, TM, 0, 0, tiled=True), beside

    stats = pl.pallas_call(
        stats_kernel,
        out_shape=jax.ShapeDtypeStruct((plane, *tile.shape), tile.dtype),
        in_specs=[whole()],
        out_specs=whole(),
    )(flat_features)
    earlier = moved(features, TM, 1)
    first_twice = jnp.concatenate([features[:1], features[:1]], axis=0)
    earlier = jnp.where(tm == 0, first_twice, earlier)
    volume = jnp.concatenate([earlier, features], axis=0)

    parts, (last, leading) = shared(stats, float(positions), (volume[:, -2:], volume[:, :2]))
    above = moved(last, "row", 1)
    below = moved(leading, "row", -1)

    border = pl.pallas_call(
        border_kernel,
        out_shape=jax.ShapeDtypeStruct((volume.shape[0], 2, 16, chans_in), jnp.bfloat16),
        in_specs=[pl.BlockSpec(memory_space=SMEM)] + [whole()] * 3,
        out_specs=whole(),
        scratch_shapes=[VMEM((chans_in // 128, 256, 128), jnp.float32)],
        compiler_params=pltpu.CompilerParams(vmem_limit_bytes=16 * MIB),
    )(place, volume, above, below)
    border = swapped(border, "col")

    copies = pl.pallas_call(
        functools.partial(hidden1_kernel, float(positions * plane), ntm),
        out_shape=jax.ShapeDtypeStruct((6, 640, chans_in), jnp.bfloat16),
        in_specs=[pl.BlockSpec(memory_space=SMEM)] + [whole()] * 7,
        out_specs=whole(),
        scratch_shapes=[VMEM((chans_in // 128, 160, 128), jnp.float32), VMEM((32, chans_in), jnp.float32)],
        compiler_params=pltpu.CompilerParams(vmem_limit_bytes=24 * MIB),
    )(place, parts, gn1_gain[None], gn1_bias[None], volume, above, below, border)

    middle, stats = pl.pallas_call(
        functools.partial(conv1_kernel, float(positions)),
        out_shape=(
            jax.ShapeDtypeStruct((288, chans_out), jnp.float32),
            jax.ShapeDtypeStruct((plane, *tile.shape), tile.dtype),
        ),
        in_specs=[whole()] + [pl.BlockSpec(memory_space=HBM)] * 2,
        out_specs=(whole(), whole()),
        scratch_shapes=[
            VMEM(copies.shape, jnp.bfloat16),
            VMEM(first.shape, jnp.bfloat16),
            pltpu.SemaphoreType.DMA((15,)),
        ],
        compiler_params=pltpu.CompilerParams(vmem_limit_bytes=60 * MIB),
    )(conv1_bias[None], copies, first)

    earlier = moved(middle, TM, 1)
    parts, _ = shared(stats, float(positions))

    copies = pl.pallas_call(
        functools.partial(hidden2_kernel, float(positions * plane), ntm),
        out_shape=jax.ShapeDtypeStruct((6, 576, chans_out), jnp.bfloat16),
        in_specs=[pl.BlockSpec(memory_space=SMEM)] + [whole()] * 5,
        out_specs=whole(),
        compiler_params=pltpu.CompilerParams(vmem_limit_bytes=16 * MIB),
    )(place, parts, gn2_gain[None], gn2_bias[None], earlier, middle)

    copies, second = lax.optimization_barrier((copies, second))
    out = pl.pallas_call(
        conv2_kernel,
        out_shape=jax.ShapeDtypeStruct((positions, chans_out), jnp.bfloat16),
        in_specs=[whole()] * 4,
        out_specs=whole(),
        scratch_shapes=[VMEM((chans_out // 128, 256, 128), jnp.float32)],
        compiler_params=pltpu.CompilerParams(vmem_limit_bytes=24 * MIB),
    )(copies, conv2_bias[None], flat_features, second)
    return out.reshape(frames, rows, cols, chans_out)


def solution(mesh):
    mesh = Mesh(mesh.devices.reshape(4, -1, *mesh.devices.shape[1:]), (*TM, "row", "col"))
    in_specs = (
        P(TM, "row", "col", None),
        P(),
        P(),
        P(None, ("row", "col"), None),
        P(),
        P(None, ("row", "col"), None),
        P(),
        P(),
        P(None, ("row", "col"), None),
        P(),
    )
    out_specs = P(TM, "row", "col", None)
    return jax.shard_map(
        per_device, mesh=mesh, in_specs=in_specs, out_specs=out_specs, check_vma=False
    )
```

```python
import functools

import jax
import jax.numpy as jnp
from jax import lax
from jax.experimental import pallas as pl
from jax.experimental.pallas import tpu as pltpu
from jax.sharding import Mesh
from jax.sharding import PartitionSpec as P

GROUPS = 32
TM = ("x", "z")
MIB = 1024 * 1024
VMEM = pltpu.VMEM
SMEM = pltpu.SMEM
HBM = pltpu.HBM


def moved(block, axis, distance):
    size = lax.axis_size(axis)
    route = [(i, i + distance) for i in range(size) if 0 <= i + distance < size]
    return lax.ppermute(block, axis, route)


def swapped(block, axis):
    return lax.ppermute(block, axis, [(0, 1), (1, 0)])


def as_rows(row):
    return jnp.concatenate([row[:, 128 * j : 128 * (j + 1)] for j in range(row.shape[1] // 128)], axis=0)


def as_row(rows):
    return jnp.concatenate([rows[j : j + 1] for j in range(rows.shape[0])], axis=1)


def packed(mean, squares):
    half = 4
    mean, squares = as_rows(mean), as_rows(squares)
    if mean.shape[0] < half:
        blank = jnp.zeros((half - mean.shape[0], 128), jnp.float32)
        mean = jnp.concatenate([mean, blank], axis=0)
        squares = jnp.concatenate([squares, blank], axis=0)
    return jnp.concatenate([mean, squares], axis=0)


def merged(parts_ref, count):
    parts = parts_ref[...]
    total = jnp.sum(parts, axis=0)
    mean = total / parts.shape[0]
    off = parts - mean[None]
    between = jnp.sum(off * off, axis=0)
    return jnp.concatenate([mean[:4], total[4:] + count * between[:4]], axis=0)


def group_average(rows, size):
    lane = lax.broadcasted_iota(jnp.int32, rows.shape, 1)
    step = 1
    while step < size:
        up, down = pltpu.roll(rows, 128 - step, 1), pltpu.roll(rows, step, 1)
        rows = rows + jnp.where((lane & step) == 0, up, down)
        step *= 2
    return rows / size


def group_moments(tile, count, size, chans):
    mean, squares = tile[:4], tile[4:]
    centre = group_average(mean, size)
    off = mean - centre
    variance = group_average(squares / count + off * off, size)
    scale = lax.rsqrt(variance + 1e-06)
    k = chans // 128
    return as_row(centre[:k]), as_row(scale[:k])


def silu_of(values, mean, scale, gain, shift):
    return jax.nn.silu((values - mean) * scale * gain + shift)


def channel_stats(values, keep, count):
    if keep is not None:
        mean = jnp.sum(jnp.where(keep, values, 0.0), axis=0, keepdims=True) / count
        off = jnp.where(keep, values - mean, 0.0)
    else:
        mean = jnp.sum(values, axis=0, keepdims=True) / count
        off = values - mean
    return packed(mean, jnp.sum(off * off, axis=0, keepdims=True))


def stats_kernel(x_ref, out_ref):
    values = x_ref[...].astype(jnp.float32)
    tile = channel_stats(values, None, float(values.shape[0]))
    out_ref[...] = jnp.broadcast_to(tile[None], out_ref.shape)


def merge_kernel(count, parts_ref, out_ref):
    out_ref[...] = jnp.broadcast_to(merged(parts_ref, count)[None], out_ref.shape)


def border_kernel(place_ref, centre_ref, above_ref, below_ref, out_ref, plain):
    row, col = place_ref[0], place_ref[1]
    pieces = plain.shape[0]

    def put(y, block):
        block = block.astype(jnp.float32)
        for j in range(pieces):
            plain[j, 16 * y : 16 * y + 16, :] = block[:, 128 * j : 128 * (j + 1)]

    plain[...] = jnp.zeros_like(plain)

    def frame(t, _):
        for y in range(2):
            put(y, jnp.where(row == 0, centre_ref[t, 0], above_ref[t, y]))
            put(y + 8, jnp.where(row == 7, centre_ref[t, 5], below_ref[t, y]))
        for y in range(6):
            put(y + 2, centre_ref[t, y])

        def column(x):
            return jnp.concatenate([plain[j, pl.ds(x, 16, stride=16), :] for j in range(pieces)], axis=1)

        for x in range(2):
            out_ref[t, x] = jnp.where(col == 0, column(14 + x), column(x)).astype(jnp.bfloat16)
        return 0

    lax.fori_loop(0, 4, frame, 0)


def hidden1_kernel(
    count, peers, place_ref, parts_ref, gain_ref, shift_ref, centre_ref, above_ref, below_ref, border_ref, out_ref, plain, side
):
    chans = centre_ref.shape[-1]
    tile = merged(parts_ref, count)
    mean, scale = group_moments(tile, count * peers, chans // GROUPS, chans)
    gain, shift = gain_ref[...], shift_ref[...]
    row, col = place_ref[0], place_ref[1]

    def normed(block):
        return silu_of(block.astype(jnp.float32), mean, scale, gain, shift)

    def put(y, block):
        for j in range(chans // 128):
            plain[j, 16 * y : 16 * y + 16, :] = block[:, 128 * j : 128 * (j + 1)]

    def frame(t, _):
        own = [normed(centre_ref[t, y]) for y in range(6)]
        for y in range(2):
            put(y, jnp.where(row == 0, own[0], normed(above_ref[t, y])))
            put(y + 8, jnp.where(row == 7, own[5], normed(below_ref[t, y])))
        for y in range(6):
            put(y + 2, own[y])
        for x in range(2):
            side[pl.ds(16 * x, 16), :] = normed(border_ref[t, x])
        for dy in range(3):

            def column(x):
                pieces = [plain[j, pl.ds(16 * dy + x, 8, stride=16), :] for j in range(chans // 128)]
                return jnp.concatenate(pieces, axis=1)

            inner = [column(x) for x in range(16)]
            outer = [side[pl.ds(16 * x + dy, 8), :] for x in range(2)]
            left = [jnp.where(col == 0, inner[0], o) for o in outer]
            right = [jnp.where(col == 0, o, inner[15]) for o in outer]
            columns = left + inner + right
            base = pl.multiple_of(t * 160, 16)
            for p in range(2):
                for i in range(10 - p):
                    pair = jnp.concatenate([columns[2 * i + p], columns[2 * i + p + 1]], axis=0)
                    out_ref[2 * dy + p, pl.ds(base + 16 * i, 16), :] = pair.astype(jnp.bfloat16)
            out_ref[2 * dy + 1, pl.ds(base + 144, 16), :] = jnp.zeros((16, chans), jnp.bfloat16)
        return 0

    lax.fori_loop(0, 4, frame, 0)


def conv1_kernel(count, bias_ref, copies_ref, gathered_ref, middle_ref, stats_ref, copies, weights, arrived):
    layouts = [pltpu.make_async_copy(copies_ref.at[i], copies.at[i], arrived.at[i]) for i in range(6)]
    fetches = [
        pltpu.make_async_copy(gathered_ref.at[3 * i : 3 * i + 3], weights.at[3 * i : 3 * i + 3], arrived.at[6 + i])
        for i in range(9)
    ]
    for dy in range(3):
        for copy in [*layouts[2 * dy : 2 * dy + 2], *fetches[dy::3]]:
            copy.start()
    middle_ref[...] = jnp.broadcast_to(bias_ref[...], middle_ref.shape)
    depth = 3 * weights.shape[1]
    for dy in range(3):
        for copy in layouts[2 * dy : 2 * dy + 2]:
            copy.wait()
        for dt in range(3):
            fetches[3 * dt + dy].wait()
            weight = weights[9 * dt + 3 * dy : 9 * dt + 3 * dy + 3].reshape(depth, weights.shape[2])

            def window(dx, dy=dy, dt=dt):
                starts = [(dt + t) * 160 + (dx // 2) * 16 for t in range(2)]
                return jnp.concatenate([copies[2 * dy + dx % 2, at : at + 144, :] for at in starts], axis=0)

            lhs = jnp.concatenate([window(dx) for dx in range(3)], axis=1)
            middle_ref[...] += jnp.dot(lhs, weight, preferred_element_type=jnp.float32)

    values = middle_ref[...]
    place = lax.broadcasted_iota(jnp.int32, values.shape, 0)
    y, x = place % 8, (place // 8) % 18
    keep = (y >= 1) & (y <= 6) & (x >= 1) & (x <= 16)
    tile = channel_stats(values, keep, count)
    stats_ref[...] = jnp.broadcast_to(tile[None], stats_ref.shape)


def hidden2_kernel(count, peers, place_ref, parts_ref, gain_ref, shift_ref, earlier_ref, middle_ref, copies):
    row, col, tm = place_ref[0], place_ref[1], place_ref[2]
    chans = middle_ref.shape[1]
    tile = merged(parts_ref, count)
    mean, scale = group_moments(tile, count * peers, chans // GROUPS, chans)
    gain, shift = gain_ref[...], shift_ref[...]
    y = lax.broadcasted_iota(jnp.int32, (8, chans), 0)
    for t in range(4):
        if t < 2:
            block = jnp.where(tm == 0, middle_ref[:144, :], earlier_ref[144 * t : 144 * t + 144, :])
        else:
            block = middle_ref[144 * (t - 2) : 144 * (t - 1), :]
        block = silu_of(block, mean, scale, gain, shift)
        columns = [block[8 * x : 8 * x + 8] for x in range(18)]
        columns[0] = jnp.where(col == 0, columns[1], columns[0])
        columns[17] = jnp.where(col == 1, columns[16], columns[17])
        for x in range(18):
            column = columns[x]
            column = jnp.where((y == 0) & (row == 0), pltpu.roll(column, 7, 0), column)
            columns[x] = jnp.where((y == 7) & (row == 7), pltpu.roll(column, 1, 0), column)
        for dy in range(3):
            rolled = columns if dy == 0 else [pltpu.roll(c, 8 - dy, 0) for c in columns]
            for p in range(2):
                for i in range(9 - p):
                    pair = jnp.concatenate([rolled[2 * i + p], rolled[2 * i + p + 1]], axis=0)
                    copies[2 * dy + p, 144 * t + 16 * i : 144 * t + 16 * i + 16, :] = pair.astype(jnp.bfloat16)


def conv2_kernel(copies, bias_ref, features_ref, weight_ref, out_ref, total):
    chans = weight_ref.shape[2]
    rows = [weight_ref[27 + h, 16 * d : 16 * d + 16, :] for d in range(chans // 16) for h in range(2)]
    skip = jnp.concatenate(rows, axis=0)
    shortcut = jnp.dot(features_ref[...], skip, preferred_element_type=jnp.float32) + bias_ref[...]
    for dt in range(3):
        for dy in range(3):
            weight = weight_ref[9 * dt + 3 * dy : 9 * dt + 3 * dy + 3].reshape(3 * chans, chans)
            for t in range(2):

                def window(dx, dy=dy, first=dt + t):
                    start = first * 144 + (dx // 2) * 16
                    return copies[2 * dy + dx % 2, start : start + 128, :]

                lhs = jnp.concatenate([window(dx) for dx in range(3)], axis=1)
                product = jnp.dot(lhs, weight, preferred_element_type=jnp.float32)
                for j in range(chans // 128):
                    part = product[:, 128 * j : 128 * (j + 1)]
                    if dt == 0 and dy == 0:
                        total[j, 128 * t : 128 * t + 128, :] = part
                    else:
                        total[j, 128 * t : 128 * t + 128, :] += part

    for t in range(2):
        for y in range(6):
            conv = [total[j, pl.ds(128 * t + y, 16, stride=8), :] for j in range(chans // 128)]
            at = (6 * t + y) * 16
            out_ref[at : at + 16, :] = (jnp.concatenate(conv, axis=1) + shortcut[at : at + 16]).astype(jnp.bfloat16)


def whole(*_):
    return pl.BlockSpec(memory_space=VMEM)


def per_device(
    features,
    gn1_gain,
    gn1_bias,
    conv1_weight,
    conv1_bias,
    skip_weight,
    gn2_gain,
    gn2_bias,
    conv2_weight,
    conv2_bias,
):
    frames, rows, cols, chans_in = features.shape
    chans_out = conv1_weight.shape[2]
    ntm, nrow, ncol = (lax.axis_size(a) for a in (TM, "row", "col"))
    tm, row, col = (lax.axis_index(a) for a in (TM, "row", "col"))
    place = jnp.stack([row, col, tm]).astype(jnp.int32)
    positions = frames * rows * cols
    plane = nrow * ncol
    flat_features = features.reshape(positions, chans_in)
    tile = jax.ShapeDtypeStruct((8, 128), jnp.float32)

    first = lax.all_gather(conv1_weight, ("row", "col"), axis=1, tiled=True)
    share = conv2_weight.shape[1]
    halves = skip_weight.reshape(2, share, chans_out)
    second = lax.all_gather(jnp.concatenate([conv2_weight, halves], axis=0), ("row", "col"), axis=1, tiled=True)

    def shared(stats, count, beside=()):
        stats = lax.all_to_all(stats, ("row", "col"), 0, 0, tiled=True)
        if beside:
            stats, beside = lax.optimization_barrier((stats, beside))
        stats = pl.pallas_call(
            functools.partial(merge_kernel, count),
            out_shape=jax.ShapeDtypeStruct((ntm, *tile.shape), tile.dtype),
            in_specs=[whole()],
            out_specs=whole(),
        )(stats)
        return lax.all_to_all(stats, TM, 0, 0, tiled=True), beside

    stats = pl.pallas_call(
        stats_kernel,
        out_shape=jax.ShapeDtypeStruct((plane, *tile.shape), tile.dtype),
        in_specs=[whole()],
        out_specs=whole(),
    )(flat_features)
    earlier = moved(features, TM, 1)
    first_twice = jnp.concatenate([features[:1], features[:1]], axis=0)
    earlier = jnp.where(tm == 0, first_twice, earlier)
    volume = jnp.concatenate([earlier, features], axis=0)

    parts, (last, leading) = shared(stats, float(positions), (volume[:, -2:], volume[:, :2]))
    above = moved(last, "row", 1)
    below = moved(leading, "row", -1)

    border = pl.pallas_call(
        border_kernel,
        out_shape=jax.ShapeDtypeStruct((volume.shape[0], 2, 16, chans_in), jnp.bfloat16),
        in_specs=[pl.BlockSpec(memory_space=SMEM)] + [whole()] * 3,
        out_specs=whole(),
        scratch_shapes=[VMEM((chans_in // 128, 288, 128), jnp.float32)],
        compiler_params=pltpu.CompilerParams(vmem_limit_bytes=16 * MIB),
    )(place, volume, above, below)
    border = swapped(border, "col")

    copies = pl.pallas_call(
        functools.partial(hidden1_kernel, float(positions * plane), ntm),
        out_shape=jax.ShapeDtypeStruct((6, 640, chans_in), jnp.bfloat16),
        in_specs=[pl.BlockSpec(memory_space=SMEM)] + [whole()] * 7,
        out_specs=whole(),
        scratch_shapes=[VMEM((chans_in // 128, 192, 128), jnp.float32), VMEM((32, chans_in), jnp.float32)],
        compiler_params=pltpu.CompilerParams(vmem_limit_bytes=24 * MIB),
    )(place, parts, gn1_gain[None], gn1_bias[None], volume, above, below, border)

    middle, stats = pl.pallas_call(
        functools.partial(conv1_kernel, float(positions)),
        out_shape=(
            jax.ShapeDtypeStruct((288, chans_out), jnp.float32),
            jax.ShapeDtypeStruct((plane, *tile.shape), tile.dtype),
        ),
        in_specs=[whole()] + [pl.BlockSpec(memory_space=HBM)] * 2,
        out_specs=(whole(), whole()),
        scratch_shapes=[
            VMEM(copies.shape, jnp.bfloat16),
            VMEM(first.shape, jnp.bfloat16),
            pltpu.SemaphoreType.DMA((15,)),
        ],
        compiler_params=pltpu.CompilerParams(vmem_limit_bytes=60 * MIB),
    )(conv1_bias[None], copies, first)

    earlier = moved(middle, TM, 1)
    parts, _ = shared(stats, float(positions))

    copies = pl.pallas_call(
        functools.partial(hidden2_kernel, float(positions * plane), ntm),
        out_shape=jax.ShapeDtypeStruct((6, 576, chans_out), jnp.bfloat16),
        in_specs=[pl.BlockSpec(memory_space=SMEM)] + [whole()] * 5,
        out_specs=whole(),
        compiler_params=pltpu.CompilerParams(vmem_limit_bytes=16 * MIB),
    )(place, parts, gn2_gain[None], gn2_bias[None], earlier, middle)

    copies, second = lax.optimization_barrier((copies, second))
    out = pl.pallas_call(
        conv2_kernel,
        out_shape=jax.ShapeDtypeStruct((positions, chans_out), jnp.bfloat16),
        in_specs=[whole()] * 4,
        out_specs=whole(),
        scratch_shapes=[VMEM((chans_out // 128, 272, 128), jnp.float32)],
        compiler_params=pltpu.CompilerParams(vmem_limit_bytes=24 * MIB),
    )(copies, conv2_bias[None], flat_features, second)
    return out.reshape(frames, rows, cols, chans_out)


def solution(mesh):
    mesh = Mesh(mesh.devices.reshape(4, -1, *mesh.devices.shape[1:]), (*TM, "row", "col"))
    in_specs = (
        P(TM, "row", "col", None),
        P(),
        P(),
        P(None, ("row", "col"), None),
        P(),
        P(None, ("row", "col"), None),
        P(),
        P(),
        P(None, ("row", "col"), None),
        P(),
    )
    out_specs = P(TM, "row", "col", None)
    return jax.shard_map(
        per_device, mesh=mesh, in_specs=in_specs, out_specs=out_specs, check_vma=False
    )
```

```python
import functools

import jax
import jax.numpy as jnp
from jax import lax
from jax.experimental import pallas as pl
from jax.experimental.pallas import tpu as pltpu
from jax.sharding import Mesh
from jax.sharding import PartitionSpec as P

GROUPS = 32
TM = ("x", "z")
MIB = 1024 * 1024
VMEM = pltpu.VMEM
SMEM = pltpu.SMEM
HBM = pltpu.HBM


def moved(block, axis, distance):
    size = lax.axis_size(axis)
    route = [(i, i + distance) for i in range(size) if 0 <= i + distance < size]
    return lax.ppermute(block, axis, route)


def swapped(block, axis):
    return lax.ppermute(block, axis, [(0, 1), (1, 0)])


def as_rows(row):
    return jnp.concatenate([row[:, 128 * j : 128 * (j + 1)] for j in range(row.shape[1] // 128)], axis=0)


def as_row(rows):
    return jnp.concatenate([rows[j : j + 1] for j in range(rows.shape[0])], axis=1)


def packed(mean, squares):
    half = 4
    mean, squares = as_rows(mean), as_rows(squares)
    if mean.shape[0] < half:
        blank = jnp.zeros((half - mean.shape[0], 128), jnp.float32)
        mean = jnp.concatenate([mean, blank], axis=0)
        squares = jnp.concatenate([squares, blank], axis=0)
    return jnp.concatenate([mean, squares], axis=0)


def merged(parts_ref, count):
    parts = parts_ref[...]
    total = jnp.sum(parts, axis=0)
    mean = total / parts.shape[0]
    off = parts - mean[None]
    between = jnp.sum(off * off, axis=0)
    return jnp.concatenate([mean[:4], total[4:] + count * between[:4]], axis=0)


def group_average(rows, size):
    lane = lax.broadcasted_iota(jnp.int32, rows.shape, 1)
    step = 1
    while step < size:
        up, down = pltpu.roll(rows, 128 - step, 1), pltpu.roll(rows, step, 1)
        rows = rows + jnp.where((lane & step) == 0, up, down)
        step *= 2
    return rows / size


def group_moments(tile, count, size, chans):
    mean, squares = tile[:4], tile[4:]
    centre = group_average(mean, size)
    off = mean - centre
    variance = group_average(squares / count + off * off, size)
    scale = lax.rsqrt(variance + 1e-06)
    k = chans // 128
    return as_row(centre[:k]), as_row(scale[:k])


def silu_of(values, mean, scale, gain, shift):
    return jax.nn.silu((values - mean) * scale * gain + shift)


def channel_stats(values, keep, count):
    if keep is not None:
        mean = jnp.sum(jnp.where(keep, values, 0.0), axis=0, keepdims=True) / count
        off = jnp.where(keep, values - mean, 0.0)
    else:
        mean = jnp.sum(values, axis=0, keepdims=True) / count
        off = values - mean
    return packed(mean, jnp.sum(off * off, axis=0, keepdims=True))


def frame_row(earlier_ref, own_ref, tm, t, y):
    if t < 2:
        return jnp.where(tm == 0, own_ref[0, y], earlier_ref[t, y])
    return own_ref[t - 2, y]


def stats_kernel(x_ref, out_ref):
    values = x_ref[...].astype(jnp.float32)
    tile = channel_stats(values, None, float(values.shape[0]))
    out_ref[...] = jnp.broadcast_to(tile[None], out_ref.shape)


def merge_kernel(count, parts_ref, out_ref):
    out_ref[...] = jnp.broadcast_to(merged(parts_ref, count)[None], out_ref.shape)


def border_kernel(place_ref, earlier_ref, own_ref, out_ref, plain):
    col, tm = place_ref[1], place_ref[2]
    pieces = plain.shape[0]
    plain[...] = jnp.zeros_like(plain)
    for t in range(4):
        for y in range(10):
            block = frame_row(earlier_ref, own_ref, tm, t, y).astype(jnp.float32)
            for j in range(pieces):
                plain[j, 16 * y : 16 * y + 16, :] = block[:, 128 * j : 128 * (j + 1)]

        def column(x):
            return jnp.concatenate([plain[j, pl.ds(x, 16, stride=16), :] for j in range(pieces)], axis=1)

        for x in range(2):
            out_ref[t, x] = jnp.where(col == 0, column(14 + x), column(x)).astype(jnp.bfloat16)


def hidden1_kernel(
    count, peers, place_ref, parts_ref, gain_ref, shift_ref, earlier_ref, own_ref, border_ref, out_ref, plain, side
):
    chans = own_ref.shape[-1]
    tile = merged(parts_ref, count)
    mean, scale = group_moments(tile, count * peers, chans // GROUPS, chans)
    gain, shift = gain_ref[...], shift_ref[...]
    col, tm = place_ref[1], place_ref[2]

    def normed(block):
        return silu_of(block.astype(jnp.float32), mean, scale, gain, shift)

    def put(y, block):
        for j in range(chans // 128):
            plain[j, 16 * y : 16 * y + 16, :] = block[:, 128 * j : 128 * (j + 1)]

    for t in range(4):
        for y in range(10):
            put(y, normed(frame_row(earlier_ref, own_ref, tm, t, y)))
        for x in range(2):
            side[pl.ds(16 * x, 16), :] = normed(border_ref[t, x])
        for dy in range(3):

            def column(x):
                pieces = [plain[j, pl.ds(16 * dy + x, 8, stride=16), :] for j in range(chans // 128)]
                return jnp.concatenate(pieces, axis=1)

            inner = [column(x) for x in range(16)]
            outer = [side[pl.ds(16 * x + dy, 8), :] for x in range(2)]
            left = [jnp.where(col == 0, inner[0], o) for o in outer]
            right = [jnp.where(col == 0, o, inner[15]) for o in outer]
            columns = left + inner + right
            base = t * 160
            for p in range(2):
                for i in range(10 - p):
                    pair = jnp.concatenate([columns[2 * i + p], columns[2 * i + p + 1]], axis=0)
                    out_ref[2 * dy + p, pl.ds(base + 16 * i, 16), :] = pair.astype(jnp.bfloat16)
            out_ref[2 * dy + 1, pl.ds(base + 144, 16), :] = jnp.zeros((16, chans), jnp.bfloat16)


def conv1_kernel(count, bias_ref, copies_ref, gathered_ref, middle_ref, stats_ref, copies, weights, arrived):
    layouts = [pltpu.make_async_copy(copies_ref.at[i], copies.at[i], arrived.at[i]) for i in range(6)]
    fetches = [
        pltpu.make_async_copy(gathered_ref.at[3 * i : 3 * i + 3], weights.at[3 * i : 3 * i + 3], arrived.at[6 + i])
        for i in range(9)
    ]
    for dy in range(3):
        for copy in [*layouts[2 * dy : 2 * dy + 2], *fetches[dy::3]]:
            copy.start()
    middle_ref[...] = jnp.broadcast_to(bias_ref[...], middle_ref.shape)
    depth = 3 * weights.shape[1]
    for dy in range(3):
        for copy in layouts[2 * dy : 2 * dy + 2]:
            copy.wait()
        for dt in range(3):
            fetches[3 * dt + dy].wait()
            weight = weights[9 * dt + 3 * dy : 9 * dt + 3 * dy + 3].reshape(depth, weights.shape[2])

            def window(dx, dy=dy, dt=dt):
                starts = [(dt + t) * 160 + (dx // 2) * 16 for t in range(2)]
                return jnp.concatenate([copies[2 * dy + dx % 2, at : at + 144, :] for at in starts], axis=0)

            lhs = jnp.concatenate([window(dx) for dx in range(3)], axis=1)
            middle_ref[...] += jnp.dot(lhs, weight, preferred_element_type=jnp.float32)

    values = middle_ref[...]
    place = lax.broadcasted_iota(jnp.int32, values.shape, 0)
    y, x = place % 8, (place // 8) % 18
    keep = (y >= 1) & (y <= 6) & (x >= 1) & (x <= 16)
    tile = channel_stats(values, keep, count)
    stats_ref[...] = jnp.broadcast_to(tile[None], stats_ref.shape)


def hidden2_kernel(count, peers, place_ref, parts_ref, gain_ref, shift_ref, earlier_ref, middle_ref, copies):
    row, col, tm = place_ref[0], place_ref[1], place_ref[2]
    chans = middle_ref.shape[1]
    tile = merged(parts_ref, count)
    mean, scale = group_moments(tile, count * peers, chans // GROUPS, chans)
    gain, shift = gain_ref[...], shift_ref[...]
    y = lax.broadcasted_iota(jnp.int32, (8, chans), 0)
    for t in range(4):
        if t < 2:
            block = jnp.where(tm == 0, middle_ref[:144, :], earlier_ref[144 * t : 144 * t + 144, :])
        else:
            block = middle_ref[144 * (t - 2) : 144 * (t - 1), :]
        block = silu_of(block, mean, scale, gain, shift)
        columns = [block[8 * x : 8 * x + 8] for x in range(18)]
        columns[0] = jnp.where(col == 0, columns[1], columns[0])
        columns[17] = jnp.where(col == 1, columns[16], columns[17])
        for x in range(18):
            column = columns[x]
            column = jnp.where((y == 0) & (row == 0), pltpu.roll(column, 7, 0), column)
            columns[x] = jnp.where((y == 7) & (row == 7), pltpu.roll(column, 1, 0), column)
        for dy in range(3):
            rolled = columns if dy == 0 else [pltpu.roll(c, 8 - dy, 0) for c in columns]
            for p in range(2):
                for i in range(9 - p):
                    pair = jnp.concatenate([rolled[2 * i + p], rolled[2 * i + p + 1]], axis=0)
                    copies[2 * dy + p, 144 * t + 16 * i : 144 * t + 16 * i + 16, :] = pair.astype(jnp.bfloat16)


def conv2_kernel(copies, bias_ref, features_ref, weight_ref, out_ref, total):
    chans = weight_ref.shape[2]
    rows = [weight_ref[27 + h, 16 * d : 16 * d + 16, :] for d in range(chans // 16) for h in range(2)]
    skip = jnp.concatenate(rows, axis=0)
    shortcut = jnp.dot(features_ref[...], skip, preferred_element_type=jnp.float32) + bias_ref[...]
    for dt in range(3):
        for dy in range(3):
            weight = weight_ref[9 * dt + 3 * dy : 9 * dt + 3 * dy + 3].reshape(3 * chans, chans)
            for t in range(2):

                def window(dx, dy=dy, first=dt + t):
                    start = first * 144 + (dx // 2) * 16
                    return copies[2 * dy + dx % 2, start : start + 128, :]

                lhs = jnp.concatenate([window(dx) for dx in range(3)], axis=1)
                product = jnp.dot(lhs, weight, preferred_element_type=jnp.float32)
                for j in range(chans // 128):
                    part = product[:, 128 * j : 128 * (j + 1)]
                    if dt == 0 and dy == 0:
                        total[j, 128 * t : 128 * t + 128, :] = part
                    else:
                        total[j, 128 * t : 128 * t + 128, :] += part

    for t in range(2):
        for y in range(6):
            conv = [total[j, pl.ds(128 * t + y, 16, stride=8), :] for j in range(chans // 128)]
            at = (6 * t + y) * 16
            out_ref[at : at + 16, :] = (jnp.concatenate(conv, axis=1) + shortcut[at : at + 16]).astype(jnp.bfloat16)


def whole(*_):
    return pl.BlockSpec(memory_space=VMEM)


def per_device(
    features,
    gn1_gain,
    gn1_bias,
    conv1_weight,
    conv1_bias,
    skip_weight,
    gn2_gain,
    gn2_bias,
    conv2_weight,
    conv2_bias,
):
    frames, rows, cols, chans_in = features.shape
    chans_out = conv1_weight.shape[2]
    ntm, nrow, ncol = (lax.axis_size(a) for a in (TM, "row", "col"))
    tm, row, col = (lax.axis_index(a) for a in (TM, "row", "col"))
    place = jnp.stack([row, col, tm]).astype(jnp.int32)
    positions = frames * rows * cols
    plane = nrow * ncol
    flat_features = features.reshape(positions, chans_in)
    tile = jax.ShapeDtypeStruct((8, 128), jnp.float32)

    first = lax.all_gather(conv1_weight, ("row", "col"), axis=1, tiled=True)
    share = conv2_weight.shape[1]
    halves = skip_weight.reshape(2, share, chans_out)
    second = lax.all_gather(jnp.concatenate([conv2_weight, halves], axis=0), ("row", "col"), axis=1, tiled=True)

    def shared(stats, count, beside=()):
        stats = lax.all_to_all(stats, ("row", "col"), 0, 0, tiled=True)
        if beside:
            stats, beside = lax.optimization_barrier((stats, beside))
        stats = pl.pallas_call(
            functools.partial(merge_kernel, count),
            out_shape=jax.ShapeDtypeStruct((ntm, *tile.shape), tile.dtype),
            in_specs=[whole()],
            out_specs=whole(),
        )(stats)
        return lax.all_to_all(stats, TM, 0, 0, tiled=True), beside

    stats = pl.pallas_call(
        stats_kernel,
        out_shape=jax.ShapeDtypeStruct((plane, *tile.shape), tile.dtype),
        in_specs=[whole()],
        out_specs=whole(),
    )(flat_features)
    above = moved(features[:, -2:], "row", 1)
    below = moved(features[:, :2], "row", -1)
    parts, (above, below) = shared(stats, float(positions), (above, below))
    above = jnp.where(row == 0, features[:, :1], above)
    below = jnp.where(row == nrow - 1, features[:, -1:], below)
    own = jnp.concatenate([above, features, below], axis=1)
    earlier = moved(own, TM, 1)
    border = pl.pallas_call(
        border_kernel,
        out_shape=jax.ShapeDtypeStruct((4, 2, 16, chans_in), jnp.bfloat16),
        in_specs=[pl.BlockSpec(memory_space=SMEM)] + [whole()] * 2,
        out_specs=whole(),
        scratch_shapes=[VMEM((chans_in // 128, 288, 128), jnp.float32)],
        compiler_params=pltpu.CompilerParams(vmem_limit_bytes=16 * MIB),
    )(place, earlier, own)
    border = swapped(border, "col")

    copies = pl.pallas_call(
        functools.partial(hidden1_kernel, float(positions * plane), ntm),
        out_shape=jax.ShapeDtypeStruct((6, 640, chans_in), jnp.bfloat16),
        in_specs=[pl.BlockSpec(memory_space=SMEM)] + [whole()] * 6,
        out_specs=whole(),
        scratch_shapes=[VMEM((chans_in // 128, 192, 128), jnp.float32), VMEM((32, chans_in), jnp.float32)],
        compiler_params=pltpu.CompilerParams(vmem_limit_bytes=24 * MIB),
    )(place, parts, gn1_gain[None], gn1_bias[None], earlier, own, border)

    middle, stats = pl.pallas_call(
        functools.partial(conv1_kernel, float(positions)),
        out_shape=(
            jax.ShapeDtypeStruct((288, chans_out), jnp.float32),
            jax.ShapeDtypeStruct((plane, *tile.shape), tile.dtype),
        ),
        in_specs=[whole()] + [pl.BlockSpec(memory_space=HBM)] * 2,
        out_specs=(whole(), whole()),
        scratch_shapes=[
            VMEM(copies.shape, jnp.bfloat16),
            VMEM(first.shape, jnp.bfloat16),
            pltpu.SemaphoreType.DMA((15,)),
        ],
        compiler_params=pltpu.CompilerParams(vmem_limit_bytes=60 * MIB),
    )(conv1_bias[None], copies, first)

    earlier = moved(middle, TM, 1)
    parts, _ = shared(stats, float(positions))

    copies = pl.pallas_call(
        functools.partial(hidden2_kernel, float(positions * plane), ntm),
        out_shape=jax.ShapeDtypeStruct((6, 576, chans_out), jnp.bfloat16),
        in_specs=[pl.BlockSpec(memory_space=SMEM)] + [whole()] * 5,
        out_specs=whole(),
        compiler_params=pltpu.CompilerParams(vmem_limit_bytes=16 * MIB),
    )(place, parts, gn2_gain[None], gn2_bias[None], earlier, middle)

    copies, second = lax.optimization_barrier((copies, second))
    out = pl.pallas_call(
        conv2_kernel,
        out_shape=jax.ShapeDtypeStruct((positions, chans_out), jnp.bfloat16),
        in_specs=[whole()] * 4,
        out_specs=whole(),
        scratch_shapes=[VMEM((chans_out // 128, 272, 128), jnp.float32)],
        compiler_params=pltpu.CompilerParams(vmem_limit_bytes=24 * MIB),
    )(copies, conv2_bias[None], flat_features, second)
    return out.reshape(frames, rows, cols, chans_out)


def solution(mesh):
    mesh = Mesh(mesh.devices.reshape(4, -1, *mesh.devices.shape[1:]), (*TM, "row", "col"))
    in_specs = (
        P(TM, "row", "col", None),
        P(),
        P(),
        P(None, ("row", "col"), None),
        P(),
        P(None, ("row", "col"), None),
        P(),
        P(),
        P(None, ("row", "col"), None),
        P(),
    )
    out_specs = P(TM, "row", "col", None)
    return jax.shard_map(
        per_device, mesh=mesh, in_specs=in_specs, out_specs=out_specs, check_vma=False
    )
```

```python
import functools

import jax
import jax.numpy as jnp
from jax import lax
from jax.experimental import pallas as pl
from jax.experimental.pallas import tpu as pltpu
from jax.sharding import Mesh
from jax.sharding import PartitionSpec as P

GROUPS = 32
TM = ("x", "z")
MIB = 1024 * 1024
VMEM = pltpu.VMEM
SMEM = pltpu.SMEM
HBM = pltpu.HBM


def moved(block, axis, distance):
    size = lax.axis_size(axis)
    route = [(i, i + distance) for i in range(size) if 0 <= i + distance < size]
    return lax.ppermute(block, axis, route)


def swapped(block, axis):
    return lax.ppermute(block, axis, [(0, 1), (1, 0)])


def as_rows(row):
    return jnp.concatenate([row[:, 128 * j : 128 * (j + 1)] for j in range(row.shape[1] // 128)], axis=0)


def as_row(rows):
    return jnp.concatenate([rows[j : j + 1] for j in range(rows.shape[0])], axis=1)


def packed(mean, squares):
    half = 4
    mean, squares = as_rows(mean), as_rows(squares)
    if mean.shape[0] < half:
        blank = jnp.zeros((half - mean.shape[0], 128), jnp.float32)
        mean = jnp.concatenate([mean, blank], axis=0)
        squares = jnp.concatenate([squares, blank], axis=0)
    return jnp.concatenate([mean, squares], axis=0)


def merged(parts_ref, count):
    parts = parts_ref[...]
    total = jnp.sum(parts, axis=0)
    mean = total / parts.shape[0]
    off = parts - mean[None]
    between = jnp.sum(off * off, axis=0)
    return jnp.concatenate([mean[:4], total[4:] + count * between[:4]], axis=0)


def group_average(rows, size):
    lane = lax.broadcasted_iota(jnp.int32, rows.shape, 1)
    step = 1
    while step < size:
        up, down = pltpu.roll(rows, 128 - step, 1), pltpu.roll(rows, step, 1)
        rows = rows + jnp.where((lane & step) == 0, up, down)
        step *= 2
    return rows / size


def group_moments(tile, count, size, chans):
    mean, squares = tile[:4], tile[4:]
    centre = group_average(mean, size)
    off = mean - centre
    variance = group_average(squares / count + off * off, size)
    scale = lax.rsqrt(variance + 1e-06)
    k = chans // 128
    return as_row(centre[:k]), as_row(scale[:k])


def silu_of(values, mean, scale, gain, shift):
    return jax.nn.silu((values - mean) * scale * gain + shift)


def channel_stats(values, keep, count):
    if keep is not None:
        mean = jnp.sum(jnp.where(keep, values, 0.0), axis=0, keepdims=True) / count
        off = jnp.where(keep, values - mean, 0.0)
    else:
        mean = jnp.sum(values, axis=0, keepdims=True) / count
        off = values - mean
    return packed(mean, jnp.sum(off * off, axis=0, keepdims=True))


def frame_row(earlier_ref, own_ref, tm, t, y):
    if t < 2:
        return jnp.where(tm == 0, own_ref[0, y], earlier_ref[t, y])
    return own_ref[t - 2, y]


def stats_kernel(x_ref, out_ref):
    values = x_ref[...].astype(jnp.float32)
    tile = channel_stats(values, None, float(values.shape[0]))
    out_ref[...] = jnp.broadcast_to(tile[None], out_ref.shape)


def merge_kernel(count, parts_ref, out_ref):
    out_ref[...] = jnp.broadcast_to(merged(parts_ref, count)[None], out_ref.shape)


def border_kernel(place_ref, earlier_ref, own_ref, out_ref, plain):
    col, tm = place_ref[1], place_ref[2]
    pieces = plain.shape[0]
    plain[...] = jnp.zeros_like(plain)
    for t in range(4):
        for y in range(10):
            block = frame_row(earlier_ref, own_ref, tm, t, y).astype(jnp.float32)
            for j in range(pieces):
                plain[j, 16 * y : 16 * y + 16, :] = block[:, 128 * j : 128 * (j + 1)]

        def column(x):
            return jnp.concatenate([plain[j, pl.ds(x, 16, stride=16), :] for j in range(pieces)], axis=1)

        for x in range(2):
            out_ref[t, x] = jnp.where(col == 0, column(14 + x), column(x)).astype(jnp.bfloat16)


def hidden1_kernel(
    count, peers, place_ref, parts_ref, gain_ref, shift_ref, earlier_ref, own_ref, border_ref, out_ref, plain, side
):
    chans = own_ref.shape[-1]
    tile = merged(parts_ref, count)
    mean, scale = group_moments(tile, count * peers, chans // GROUPS, chans)
    gain, shift = gain_ref[...], shift_ref[...]
    col, tm = place_ref[1], place_ref[2]

    def normed(block):
        return silu_of(block.astype(jnp.float32), mean, scale, gain, shift)

    def put(y, block):
        for j in range(chans // 128):
            plain[j, 16 * y : 16 * y + 16, :] = block[:, 128 * j : 128 * (j + 1)]

    for t in range(4):
        for y in range(10):
            put(y, normed(frame_row(earlier_ref, own_ref, tm, t, y)))
        for x in range(2):
            side[pl.ds(16 * x, 16), :] = normed(border_ref[t, x])
        for dy in range(3):

            def column(x):
                pieces = [plain[j, pl.ds(16 * dy + x, 8, stride=16), :] for j in range(chans // 128)]
                return jnp.concatenate(pieces, axis=1)

            inner = [column(x) for x in range(16)]
            outer = [side[pl.ds(16 * x + dy, 8), :] for x in range(2)]
            left = [jnp.where(col == 0, inner[0], o) for o in outer]
            right = [jnp.where(col == 0, o, inner[15]) for o in outer]
            columns = left + inner + right
            base = t * 160
            for i in range(10):
                pair = jnp.concatenate([columns[2 * i], columns[2 * i + 1]], axis=0)
                out_ref[dy, pl.ds(base + 16 * i, 16), :] = pair.astype(jnp.bfloat16)


def conv1_kernel(count, bias_ref, copies_ref, gathered_ref, middle_ref, stats_ref, total, copies, weights, arrived):
    layouts = [pltpu.make_async_copy(copies_ref.at[dy], copies.at[dy], arrived.at[dy]) for dy in range(3)]
    fetches = [
        pltpu.make_async_copy(gathered_ref.at[3 * i : 3 * i + 3], weights.at[3 * i : 3 * i + 3], arrived.at[3 + i])
        for i in range(9)
    ]
    for dy in range(3):
        for copy in [layouts[dy], *fetches[dy::3]]:
            copy.start()
    for dy in range(3):
        for copy in [layouts[dy], *fetches[dy::3]]:
            copy.wait()
        lhs = jnp.concatenate([copies[dy, 160 * dt : 160 * dt + 320, :] for dt in range(3)], axis=1)
        for dx in range(3):
            weight = jnp.concatenate([weights[9 * dt + 3 * dy + dx] for dt in range(3)], axis=0)
            product = jnp.dot(lhs, weight, preferred_element_type=jnp.float32)
            if dy == 0:
                total[dx] = product
            else:
                total[dx] += product

    frames = []
    for t in range(2):
        parts = [total[dx, 160 * t + 8 * dx : 160 * t + 8 * dx + 144, :] for dx in range(3)]
        frames.append(parts[0] + parts[1] + parts[2] + bias_ref[...])
    values = jnp.concatenate(frames, axis=0)
    middle_ref[...] = values
    place = lax.broadcasted_iota(jnp.int32, values.shape, 0)
    y, x = place % 8, (place // 8) % 18
    keep = (y >= 1) & (y <= 6) & (x >= 1) & (x <= 16)
    tile = channel_stats(values, keep, count)
    stats_ref[...] = jnp.broadcast_to(tile[None], stats_ref.shape)


def hidden2_kernel(count, peers, place_ref, parts_ref, gain_ref, shift_ref, earlier_ref, middle_ref, copies):
    row, col, tm = place_ref[0], place_ref[1], place_ref[2]
    chans = middle_ref.shape[1]
    tile = merged(parts_ref, count)
    mean, scale = group_moments(tile, count * peers, chans // GROUPS, chans)
    gain, shift = gain_ref[...], shift_ref[...]
    y = lax.broadcasted_iota(jnp.int32, (8, chans), 0)
    for t in range(4):
        if t < 2:
            block = jnp.where(tm == 0, middle_ref[:144, :], earlier_ref[144 * t : 144 * t + 144, :])
        else:
            block = middle_ref[144 * (t - 2) : 144 * (t - 1), :]
        block = silu_of(block, mean, scale, gain, shift)
        columns = [block[8 * x : 8 * x + 8] for x in range(18)]
        columns[0] = jnp.where(col == 0, columns[1], columns[0])
        columns[17] = jnp.where(col == 1, columns[16], columns[17])
        for x in range(18):
            column = columns[x]
            column = jnp.where((y == 0) & (row == 0), pltpu.roll(column, 7, 0), column)
            columns[x] = jnp.where((y == 7) & (row == 7), pltpu.roll(column, 1, 0), column)
        for dy in range(3):
            rolled = columns if dy == 0 else [pltpu.roll(c, 8 - dy, 0) for c in columns]
            for p in range(2):
                for i in range(9 - p):
                    pair = jnp.concatenate([rolled[2 * i + p], rolled[2 * i + p + 1]], axis=0)
                    copies[2 * dy + p, 144 * t + 16 * i : 144 * t + 16 * i + 16, :] = pair.astype(jnp.bfloat16)


def conv2_kernel(copies, bias_ref, features_ref, weight_ref, out_ref, total):
    chans = weight_ref.shape[2]
    rows = [weight_ref[27 + h, 16 * d : 16 * d + 16, :] for d in range(chans // 16) for h in range(2)]
    skip = jnp.concatenate(rows, axis=0)
    shortcut = jnp.dot(features_ref[...], skip, preferred_element_type=jnp.float32) + bias_ref[...]
    for dt in range(3):
        for dy in range(3):
            weight = weight_ref[9 * dt + 3 * dy : 9 * dt + 3 * dy + 3].reshape(3 * chans, chans)
            for t in range(2):

                def window(dx, dy=dy, first=dt + t):
                    start = first * 144 + (dx // 2) * 16
                    return copies[2 * dy + dx % 2, start : start + 128, :]

                lhs = jnp.concatenate([window(dx) for dx in range(3)], axis=1)
                product = jnp.dot(lhs, weight, preferred_element_type=jnp.float32)
                for j in range(chans // 128):
                    part = product[:, 128 * j : 128 * (j + 1)]
                    if dt == 0 and dy == 0:
                        total[j, 128 * t : 128 * t + 128, :] = part
                    else:
                        total[j, 128 * t : 128 * t + 128, :] += part

    for t in range(2):
        for y in range(6):
            conv = [total[j, pl.ds(128 * t + y, 16, stride=8), :] for j in range(chans // 128)]
            at = (6 * t + y) * 16
            out_ref[at : at + 16, :] = (jnp.concatenate(conv, axis=1) + shortcut[at : at + 16]).astype(jnp.bfloat16)


def whole(*_):
    return pl.BlockSpec(memory_space=VMEM)


def per_device(
    features,
    gn1_gain,
    gn1_bias,
    conv1_weight,
    conv1_bias,
    skip_weight,
    gn2_gain,
    gn2_bias,
    conv2_weight,
    conv2_bias,
):
    frames, rows, cols, chans_in = features.shape
    chans_out = conv1_weight.shape[2]
    ntm, nrow, ncol = (lax.axis_size(a) for a in (TM, "row", "col"))
    tm, row, col = (lax.axis_index(a) for a in (TM, "row", "col"))
    place = jnp.stack([row, col, tm]).astype(jnp.int32)
    positions = frames * rows * cols
    plane = nrow * ncol
    flat_features = features.reshape(positions, chans_in)
    tile = jax.ShapeDtypeStruct((8, 128), jnp.float32)

    first = lax.all_gather(conv1_weight, ("row", "col"), axis=1, tiled=True)
    share = conv2_weight.shape[1]
    halves = skip_weight.reshape(2, share, chans_out)
    second = lax.all_gather(jnp.concatenate([conv2_weight, halves], axis=0), ("row", "col"), axis=1, tiled=True)

    def shared(stats, count, beside=()):
        stats = lax.all_to_all(stats, ("row", "col"), 0, 0, tiled=True)
        if beside:
            stats, beside = lax.optimization_barrier((stats, beside))
        stats = pl.pallas_call(
            functools.partial(merge_kernel, count),
            out_shape=jax.ShapeDtypeStruct((ntm, *tile.shape), tile.dtype),
            in_specs=[whole()],
            out_specs=whole(),
        )(stats)
        return lax.all_to_all(stats, TM, 0, 0, tiled=True), beside

    stats = pl.pallas_call(
        stats_kernel,
        out_shape=jax.ShapeDtypeStruct((plane, *tile.shape), tile.dtype),
        in_specs=[whole()],
        out_specs=whole(),
    )(flat_features)
    above = moved(features[:, -2:], "row", 1)
    below = moved(features[:, :2], "row", -1)
    parts, (above, below) = shared(stats, float(positions), (above, below))
    above = jnp.where(row == 0, features[:, :1], above)
    below = jnp.where(row == nrow - 1, features[:, -1:], below)
    own = jnp.concatenate([above, features, below], axis=1)
    earlier = moved(own, TM, 1)
    border = pl.pallas_call(
        border_kernel,
        out_shape=jax.ShapeDtypeStruct((4, 2, 16, chans_in), jnp.bfloat16),
        in_specs=[pl.BlockSpec(memory_space=SMEM)] + [whole()] * 2,
        out_specs=whole(),
        scratch_shapes=[VMEM((chans_in // 128, 288, 128), jnp.float32)],
        compiler_params=pltpu.CompilerParams(vmem_limit_bytes=16 * MIB),
    )(place, earlier, own)
    border = swapped(border, "col")

    copies = pl.pallas_call(
        functools.partial(hidden1_kernel, float(positions * plane), ntm),
        out_shape=jax.ShapeDtypeStruct((3, 640, chans_in), jnp.bfloat16),
        in_specs=[pl.BlockSpec(memory_space=SMEM)] + [whole()] * 6,
        out_specs=whole(),
        scratch_shapes=[VMEM((chans_in // 128, 192, 128), jnp.float32), VMEM((32, chans_in), jnp.float32)],
        compiler_params=pltpu.CompilerParams(vmem_limit_bytes=24 * MIB),
    )(place, parts, gn1_gain[None], gn1_bias[None], earlier, own, border)

    middle, stats = pl.pallas_call(
        functools.partial(conv1_kernel, float(positions)),
        out_shape=(
            jax.ShapeDtypeStruct((288, chans_out), jnp.float32),
            jax.ShapeDtypeStruct((plane, *tile.shape), tile.dtype),
        ),
        in_specs=[whole()] + [pl.BlockSpec(memory_space=HBM)] * 2,
        out_specs=(whole(), whole()),
        scratch_shapes=[
            VMEM((3, 320, chans_out), jnp.float32),
            VMEM(copies.shape, jnp.bfloat16),
            VMEM(first.shape, jnp.bfloat16),
            pltpu.SemaphoreType.DMA((15,)),
        ],
        compiler_params=pltpu.CompilerParams(vmem_limit_bytes=60 * MIB),
    )(conv1_bias[None], copies, first)

    earlier = moved(middle, TM, 1)
    parts, _ = shared(stats, float(positions))

    copies = pl.pallas_call(
        functools.partial(hidden2_kernel, float(positions * plane), ntm),
        out_shape=jax.ShapeDtypeStruct((6, 576, chans_out), jnp.bfloat16),
        in_specs=[pl.BlockSpec(memory_space=SMEM)] + [whole()] * 5,
        out_specs=whole(),
        compiler_params=pltpu.CompilerParams(vmem_limit_bytes=16 * MIB),
    )(place, parts, gn2_gain[None], gn2_bias[None], earlier, middle)

    copies, second = lax.optimization_barrier((copies, second))
    out = pl.pallas_call(
        conv2_kernel,
        out_shape=jax.ShapeDtypeStruct((positions, chans_out), jnp.bfloat16),
        in_specs=[whole()] * 4,
        out_specs=whole(),
        scratch_shapes=[VMEM((chans_out // 128, 272, 128), jnp.float32)],
        compiler_params=pltpu.CompilerParams(vmem_limit_bytes=24 * MIB),
    )(copies, conv2_bias[None], flat_features, second)
    return out.reshape(frames, rows, cols, chans_out)


def solution(mesh):
    mesh = Mesh(mesh.devices.reshape(4, -1, *mesh.devices.shape[1:]), (*TM, "row", "col"))
    in_specs = (
        P(TM, "row", "col", None),
        P(),
        P(),
        P(None, ("row", "col"), None),
        P(),
        P(None, ("row", "col"), None),
        P(),
        P(),
        P(None, ("row", "col"), None),
        P(),
    )
    out_specs = P(TM, "row", "col", None)
    return jax.shard_map(
        per_device, mesh=mesh, in_specs=in_specs, out_specs=out_specs, check_vma=False
    )
```

```python
import functools

import jax
import jax.numpy as jnp
from jax import lax
from jax.experimental import pallas as pl
from jax.experimental.pallas import tpu as pltpu
from jax.sharding import Mesh
from jax.sharding import PartitionSpec as P

GROUPS = 32
TM = ("x", "z")
MIB = 1024 * 1024
VMEM = pltpu.VMEM
SMEM = pltpu.SMEM
HBM = pltpu.HBM


def moved(block, axis, distance):
    size = lax.axis_size(axis)
    route = [(i, i + distance) for i in range(size) if 0 <= i + distance < size]
    return lax.ppermute(block, axis, route)


def swapped(block, axis):
    return lax.ppermute(block, axis, [(0, 1), (1, 0)])


def as_rows(row):
    return jnp.concatenate([row[:, 128 * j : 128 * (j + 1)] for j in range(row.shape[1] // 128)], axis=0)


def as_row(rows):
    return jnp.concatenate([rows[j : j + 1] for j in range(rows.shape[0])], axis=1)


def packed(mean, squares):
    half = 4
    mean, squares = as_rows(mean), as_rows(squares)
    if mean.shape[0] < half:
        blank = jnp.zeros((half - mean.shape[0], 128), jnp.float32)
        mean = jnp.concatenate([mean, blank], axis=0)
        squares = jnp.concatenate([squares, blank], axis=0)
    return jnp.concatenate([mean, squares], axis=0)


def merged(parts_ref, count):
    parts = parts_ref[...]
    total = jnp.sum(parts, axis=0)
    mean = total / parts.shape[0]
    off = parts - mean[None]
    between = jnp.sum(off * off, axis=0)
    return jnp.concatenate([mean[:4], total[4:] + count * between[:4]], axis=0)


def group_average(rows, size):
    lane = lax.broadcasted_iota(jnp.int32, rows.shape, 1)
    step = 1
    while step < size:
        up, down = pltpu.roll(rows, 128 - step, 1), pltpu.roll(rows, step, 1)
        rows = rows + jnp.where((lane & step) == 0, up, down)
        step *= 2
    return rows / size


def group_moments(tile, count, size, chans):
    mean, squares = tile[:4], tile[4:]
    centre = group_average(mean, size)
    off = mean - centre
    variance = group_average(squares / count + off * off, size)
    scale = lax.rsqrt(variance + 1e-06)
    k = chans // 128
    return as_row(centre[:k]), as_row(scale[:k])


def silu_of(values, mean, scale, gain, shift):
    return jax.nn.silu((values - mean) * scale * gain + shift)


def channel_stats(values, keep, count):
    if keep is not None:
        mean = jnp.sum(jnp.where(keep, values, 0.0), axis=0, keepdims=True) / count
        off = jnp.where(keep, values - mean, 0.0)
    else:
        mean = jnp.sum(values, axis=0, keepdims=True) / count
        off = values - mean
    return packed(mean, jnp.sum(off * off, axis=0, keepdims=True))


def frame_row(earlier_ref, own_ref, tm, t, y):
    if t < 2:
        return jnp.where(tm == 0, own_ref[0, y], earlier_ref[t, y])
    return own_ref[t - 2, y]


def stats_kernel(x_ref, out_ref):
    values = x_ref[...].astype(jnp.float32)
    tile = channel_stats(values, None, float(values.shape[0]))
    out_ref[...] = jnp.broadcast_to(tile[None], out_ref.shape)


def merge_kernel(count, parts_ref, out_ref):
    out_ref[...] = jnp.broadcast_to(merged(parts_ref, count)[None], out_ref.shape)


def border_kernel(place_ref, earlier_ref, own_ref, out_ref, plain):
    col, tm = place_ref[1], place_ref[2]
    pieces = plain.shape[0]
    plain[...] = jnp.zeros_like(plain)
    for t in range(4):
        for y in range(10):
            block = frame_row(earlier_ref, own_ref, tm, t, y).astype(jnp.float32)
            for j in range(pieces):
                plain[j, 16 * y : 16 * y + 16, :] = block[:, 128 * j : 128 * (j + 1)]

        def column(x):
            return jnp.concatenate([plain[j, pl.ds(x, 16, stride=16), :] for j in range(pieces)], axis=1)

        for x in range(2):
            out_ref[t, x] = jnp.where(col == 0, column(14 + x), column(x)).astype(jnp.bfloat16)


def hidden1_kernel(
    count, peers, place_ref, parts_ref, gain_ref, shift_ref, earlier_ref, own_ref, border_ref, out_ref, plain, side
):
    chans = own_ref.shape[-1]
    tile = merged(parts_ref, count)
    mean, scale = group_moments(tile, count * peers, chans // GROUPS, chans)
    gain, shift = gain_ref[...], shift_ref[...]
    col, tm = place_ref[1], place_ref[2]

    def normed(block):
        return silu_of(block.astype(jnp.float32), mean, scale, gain, shift)

    def put(y, block):
        for j in range(chans // 128):
            plain[j, 16 * y : 16 * y + 16, :] = block[:, 128 * j : 128 * (j + 1)]

    for t in range(4):
        for y in range(10):
            put(y, normed(frame_row(earlier_ref, own_ref, tm, t, y)))
        for x in range(2):
            side[pl.ds(16 * x, 16), :] = normed(border_ref[t, x])
        for dy in range(3):

            def column(x):
                pieces = [plain[j, pl.ds(16 * dy + x, 8, stride=16), :] for j in range(chans // 128)]
                return jnp.concatenate(pieces, axis=1)

            inner = [column(x) for x in range(16)]
            outer = [side[pl.ds(16 * x + dy, 8), :] for x in range(2)]
            left = [jnp.where(col == 0, inner[0], o) for o in outer]
            right = [jnp.where(col == 0, o, inner[15]) for o in outer]
            columns = left + inner + right
            base = t * 160
            for p in range(2):
                for i in range(10 - p):
                    pair = jnp.concatenate([columns[2 * i + p], columns[2 * i + p + 1]], axis=0)
                    out_ref[2 * dy + p, pl.ds(base + 16 * i, 16), :] = pair.astype(jnp.bfloat16)
            out_ref[2 * dy + 1, pl.ds(base + 144, 16), :] = jnp.zeros((16, chans), jnp.bfloat16)


def conv1_kernel(count, bias_ref, copies_ref, gathered_ref, middle_ref, stats_ref, copies, weights, arrived):
    layouts = [pltpu.make_async_copy(copies_ref.at[i], copies.at[i], arrived.at[i]) for i in range(6)]
    fetches = [
        pltpu.make_async_copy(gathered_ref.at[3 * i : 3 * i + 3], weights.at[3 * i : 3 * i + 3], arrived.at[6 + i])
        for i in range(9)
    ]
    for dy in range(3):
        for copy in [*layouts[2 * dy : 2 * dy + 2], *fetches[dy::3]]:
            copy.start()
    middle_ref[...] = jnp.broadcast_to(bias_ref[...], middle_ref.shape)
    depth = 3 * weights.shape[1]
    for dy in range(3):
        for copy in layouts[2 * dy : 2 * dy + 2]:
            copy.wait()
        for dt in range(3):
            fetches[3 * dt + dy].wait()
            weight = weights[9 * dt + 3 * dy : 9 * dt + 3 * dy + 3].reshape(depth, weights.shape[2])

            def window(dx, dy=dy, dt=dt):
                starts = [(dt + t) * 160 + (dx // 2) * 16 for t in range(2)]
                return jnp.concatenate([copies[2 * dy + dx % 2, at : at + 144, :] for at in starts], axis=0)

            lhs = jnp.concatenate([window(dx) for dx in range(3)], axis=1)
            middle_ref[...] += jnp.dot(lhs, weight, preferred_element_type=jnp.float32)

    values = middle_ref[...]
    place = lax.broadcasted_iota(jnp.int32, values.shape, 0)
    y, x = place % 8, (place // 8) % 18
    keep = (y >= 1) & (y <= 6) & (x >= 1) & (x <= 16)
    tile = channel_stats(values, keep, count)
    stats_ref[...] = jnp.broadcast_to(tile[None], stats_ref.shape)


def hidden2_kernel(count, peers, place_ref, parts_ref, gain_ref, shift_ref, earlier_ref, middle_ref, copies):
    row, col, tm = place_ref[0], place_ref[1], place_ref[2]
    chans = middle_ref.shape[1]
    tile = merged(parts_ref, count)
    mean, scale = group_moments(tile, count * peers, chans // GROUPS, chans)
    gain, shift = gain_ref[...], shift_ref[...]
    y = lax.broadcasted_iota(jnp.int32, (8, chans), 0)
    for t in range(4):
        if t < 2:
            block = jnp.where(tm == 0, middle_ref[:144, :], earlier_ref[144 * t : 144 * t + 144, :])
        else:
            block = middle_ref[144 * (t - 2) : 144 * (t - 1), :]
        block = silu_of(block, mean, scale, gain, shift)
        columns = [block[8 * x : 8 * x + 8] for x in range(18)]
        columns[0] = jnp.where(col == 0, columns[1], columns[0])
        columns[17] = jnp.where(col == 1, columns[16], columns[17])
        for x in range(18):
            column = columns[x]
            column = jnp.where((y == 0) & (row == 0), pltpu.roll(column, 7, 0), column)
            columns[x] = jnp.where((y == 7) & (row == 7), pltpu.roll(column, 1, 0), column)
        for dy in range(3):
            rolled = columns if dy == 0 else [pltpu.roll(c, 8 - dy, 0) for c in columns]
            for p in range(2):
                for i in range(9 - p):
                    pair = jnp.concatenate([rolled[2 * i + p], rolled[2 * i + p + 1]], axis=0)
                    copies[2 * dy + p, 144 * t + 16 * i : 144 * t + 16 * i + 16, :] = pair.astype(jnp.bfloat16)


def conv2_kernel(copies, bias_ref, features_ref, weight_ref, out_ref, total):
    chans = weight_ref.shape[2]
    rows = [weight_ref[27 + h, 16 * d : 16 * d + 16, :] for d in range(chans // 16) for h in range(2)]
    skip = jnp.concatenate(rows, axis=0)
    shortcut = jnp.dot(features_ref[...], skip, preferred_element_type=jnp.float32) + bias_ref[...]
    for dt in range(3):
        for dy in range(3):
            weight = weight_ref[9 * dt + 3 * dy : 9 * dt + 3 * dy + 3].reshape(3 * chans, chans)

            def window(dx, dy=dy, dt=dt):
                starts = [(dt + t) * 144 + (dx // 2) * 16 for t in range(2)]
                return jnp.concatenate([copies[2 * dy + dx % 2, at : at + 128, :] for at in starts], axis=0)

            lhs = jnp.concatenate([window(dx) for dx in range(3)], axis=1)
            product = jnp.dot(lhs, weight, preferred_element_type=jnp.float32)
            for j in range(chans // 128):
                part = product[:, 128 * j : 128 * (j + 1)]
                if dt == 0 and dy == 0:
                    total[j, :256, :] = part
                else:
                    total[j, :256, :] += part

    for t in range(2):
        for y in range(6):
            conv = [total[j, pl.ds(128 * t + y, 16, stride=8), :] for j in range(chans // 128)]
            at = (6 * t + y) * 16
            out_ref[at : at + 16, :] = (jnp.concatenate(conv, axis=1) + shortcut[at : at + 16]).astype(jnp.bfloat16)


def whole(*_):
    return pl.BlockSpec(memory_space=VMEM)


def per_device(
    features,
    gn1_gain,
    gn1_bias,
    conv1_weight,
    conv1_bias,
    skip_weight,
    gn2_gain,
    gn2_bias,
    conv2_weight,
    conv2_bias,
):
    frames, rows, cols, chans_in = features.shape
    chans_out = conv1_weight.shape[2]
    ntm, nrow, ncol = (lax.axis_size(a) for a in (TM, "row", "col"))
    tm, row, col = (lax.axis_index(a) for a in (TM, "row", "col"))
    place = jnp.stack([row, col, tm]).astype(jnp.int32)
    positions = frames * rows * cols
    plane = nrow * ncol
    flat_features = features.reshape(positions, chans_in)
    tile = jax.ShapeDtypeStruct((8, 128), jnp.float32)

    first = lax.all_gather(conv1_weight, ("row", "col"), axis=1, tiled=True)
    share = conv2_weight.shape[1]
    halves = skip_weight.reshape(2, share, chans_out)
    second = lax.all_gather(jnp.concatenate([conv2_weight, halves], axis=0), ("row", "col"), axis=1, tiled=True)

    def shared(stats, count, beside=()):
        stats = lax.all_to_all(stats, ("row", "col"), 0, 0, tiled=True)
        if beside:
            stats, beside = lax.optimization_barrier((stats, beside))
        stats = pl.pallas_call(
            functools.partial(merge_kernel, count),
            out_shape=jax.ShapeDtypeStruct((ntm, *tile.shape), tile.dtype),
            in_specs=[whole()],
            out_specs=whole(),
        )(stats)
        return lax.all_to_all(stats, TM, 0, 0, tiled=True), beside

    stats = pl.pallas_call(
        stats_kernel,
        out_shape=jax.ShapeDtypeStruct((plane, *tile.shape), tile.dtype),
        in_specs=[whole()],
        out_specs=whole(),
    )(flat_features)
    above = moved(features[:, -2:], "row", 1)
    below = moved(features[:, :2], "row", -1)
    parts, (above, below) = shared(stats, float(positions), (above, below))
    above = jnp.where(row == 0, features[:, :1], above)
    below = jnp.where(row == nrow - 1, features[:, -1:], below)
    own = jnp.concatenate([above, features, below], axis=1)
    earlier = moved(own, TM, 1)
    border = pl.pallas_call(
        border_kernel,
        out_shape=jax.ShapeDtypeStruct((4, 2, 16, chans_in), jnp.bfloat16),
        in_specs=[pl.BlockSpec(memory_space=SMEM)] + [whole()] * 2,
        out_specs=whole(),
        scratch_shapes=[VMEM((chans_in // 128, 288, 128), jnp.float32)],
        compiler_params=pltpu.CompilerParams(vmem_limit_bytes=16 * MIB),
    )(place, earlier, own)
    border = swapped(border, "col")

    copies = pl.pallas_call(
        functools.partial(hidden1_kernel, float(positions * plane), ntm),
        out_shape=jax.ShapeDtypeStruct((6, 640, chans_in), jnp.bfloat16),
        in_specs=[pl.BlockSpec(memory_space=SMEM)] + [whole()] * 6,
        out_specs=whole(),
        scratch_shapes=[VMEM((chans_in // 128, 192, 128), jnp.float32), VMEM((32, chans_in), jnp.float32)],
        compiler_params=pltpu.CompilerParams(vmem_limit_bytes=24 * MIB),
    )(place, parts, gn1_gain[None], gn1_bias[None], earlier, own, border)

    middle, stats = pl.pallas_call(
        functools.partial(conv1_kernel, float(positions)),
        out_shape=(
            jax.ShapeDtypeStruct((288, chans_out), jnp.float32),
            jax.ShapeDtypeStruct((plane, *tile.shape), tile.dtype),
        ),
        in_specs=[whole()] + [pl.BlockSpec(memory_space=HBM)] * 2,
        out_specs=(whole(), whole()),
        scratch_shapes=[
            VMEM(copies.shape, jnp.bfloat16),
            VMEM(first.shape, jnp.bfloat16),
            pltpu.SemaphoreType.DMA((15,)),
        ],
        compiler_params=pltpu.CompilerParams(vmem_limit_bytes=60 * MIB),
    )(conv1_bias[None], copies, first)

    earlier = moved(middle, TM, 1)
    parts, _ = shared(stats, float(positions))

    copies = pl.pallas_call(
        functools.partial(hidden2_kernel, float(positions * plane), ntm),
        out_shape=jax.ShapeDtypeStruct((6, 576, chans_out), jnp.bfloat16),
        in_specs=[pl.BlockSpec(memory_space=SMEM)] + [whole()] * 5,
        out_specs=whole(),
        compiler_params=pltpu.CompilerParams(vmem_limit_bytes=16 * MIB),
    )(place, parts, gn2_gain[None], gn2_bias[None], earlier, middle)

    copies, second = lax.optimization_barrier((copies, second))
    out = pl.pallas_call(
        conv2_kernel,
        out_shape=jax.ShapeDtypeStruct((positions, chans_out), jnp.bfloat16),
        in_specs=[whole()] * 4,
        out_specs=whole(),
        scratch_shapes=[VMEM((chans_out // 128, 272, 128), jnp.float32)],
        compiler_params=pltpu.CompilerParams(vmem_limit_bytes=24 * MIB),
    )(copies, conv2_bias[None], flat_features, second)
    return out.reshape(frames, rows, cols, chans_out)


def solution(mesh):
    mesh = Mesh(mesh.devices.reshape(4, -1, *mesh.devices.shape[1:]), (*TM, "row", "col"))
    in_specs = (
        P(TM, "row", "col", None),
        P(),
        P(),
        P(None, ("row", "col"), None),
        P(),
        P(None, ("row", "col"), None),
        P(),
        P(),
        P(None, ("row", "col"), None),
        P(),
    )
    out_specs = P(TM, "row", "col", None)
    return jax.shard_map(
        per_device, mesh=mesh, in_specs=in_specs, out_specs=out_specs, check_vma=False
    )
```

```python
import functools

import jax
import jax.numpy as jnp
from jax import lax
from jax.experimental import pallas as pl
from jax.experimental.pallas import tpu as pltpu
from jax.sharding import Mesh
from jax.sharding import PartitionSpec as P

GROUPS = 32
TM = ("x", "z")
MIB = 1024 * 1024
VMEM = pltpu.VMEM
SMEM = pltpu.SMEM
HBM = pltpu.HBM


def moved(block, axis, distance):
    size = lax.axis_size(axis)
    route = [(i, i + distance) for i in range(size) if 0 <= i + distance < size]
    return lax.ppermute(block, axis, route)


def swapped(block, axis):
    return lax.ppermute(block, axis, [(0, 1), (1, 0)])


def as_rows(row):
    return jnp.concatenate([row[:, 128 * j : 128 * (j + 1)] for j in range(row.shape[1] // 128)], axis=0)


def as_row(rows):
    return jnp.concatenate([rows[j : j + 1] for j in range(rows.shape[0])], axis=1)


def packed(mean, squares):
    half = 4
    mean, squares = as_rows(mean), as_rows(squares)
    if mean.shape[0] < half:
        blank = jnp.zeros((half - mean.shape[0], 128), jnp.float32)
        mean = jnp.concatenate([mean, blank], axis=0)
        squares = jnp.concatenate([squares, blank], axis=0)
    return jnp.concatenate([mean, squares], axis=0)


def merged(parts_ref, count):
    parts = parts_ref[...]
    total = jnp.sum(parts, axis=0)
    mean = total / parts.shape[0]
    off = parts - mean[None]
    between = jnp.sum(off * off, axis=0)
    return jnp.concatenate([mean[:4], total[4:] + count * between[:4]], axis=0)


def group_average(rows, size):
    lane = lax.broadcasted_iota(jnp.int32, rows.shape, 1)
    step = 1
    while step < size:
        up, down = pltpu.roll(rows, 128 - step, 1), pltpu.roll(rows, step, 1)
        rows = rows + jnp.where((lane & step) == 0, up, down)
        step *= 2
    return rows / size


def group_moments(tile, count, size, chans):
    mean, squares = tile[:4], tile[4:]
    centre = group_average(mean, size)
    off = mean - centre
    variance = group_average(squares / count + off * off, size)
    scale = lax.rsqrt(variance + 1e-06)
    k = chans // 128
    return as_row(centre[:k]), as_row(scale[:k])


def silu_of(values, mean, scale, gain, shift):
    return jax.nn.silu((values - mean) * scale * gain + shift)


def channel_stats(values, keep, count):
    if keep is not None:
        mean = jnp.sum(jnp.where(keep, values, 0.0), axis=0, keepdims=True) / count
        off = jnp.where(keep, values - mean, 0.0)
    else:
        mean = jnp.sum(values, axis=0, keepdims=True) / count
        off = values - mean
    return packed(mean, jnp.sum(off * off, axis=0, keepdims=True))


def frame_row(earlier_ref, own_ref, tm, t, y):
    if t < 2:
        return jnp.where(tm == 0, own_ref[0, y], earlier_ref[t, y])
    return own_ref[t - 2, y]


def stats_kernel(x_ref, out_ref):
    values = x_ref[...].astype(jnp.float32)
    tile = channel_stats(values, None, float(values.shape[0]))
    out_ref[...] = jnp.broadcast_to(tile[None], out_ref.shape)


def merge_kernel(count, parts_ref, out_ref):
    out_ref[...] = jnp.broadcast_to(merged(parts_ref, count)[None], out_ref.shape)


def border_kernel(place_ref, earlier_ref, own_ref, out_ref, plain):
    col, tm = place_ref[1], place_ref[2]
    pieces = plain.shape[0]
    plain[...] = jnp.zeros_like(plain)
    for t in range(4):
        for y in range(10):
            block = frame_row(earlier_ref, own_ref, tm, t, y).astype(jnp.float32)
            for j in range(pieces):
                plain[j, 16 * y : 16 * y + 16, :] = block[:, 128 * j : 128 * (j + 1)]

        def column(x):
            return jnp.concatenate([plain[j, pl.ds(x, 16, stride=16), :] for j in range(pieces)], axis=1)

        for x in range(2):
            out_ref[t, x] = jnp.where(col == 0, column(14 + x), column(x)).astype(jnp.bfloat16)


def hidden1_kernel(
    count, peers, place_ref, parts_ref, gain_ref, shift_ref, earlier_ref, own_ref, border_ref, out_ref, plain, side
):
    chans = own_ref.shape[-1]
    tile = merged(parts_ref, count)
    mean, scale = group_moments(tile, count * peers, chans // GROUPS, chans)
    gain, shift = gain_ref[...], shift_ref[...]
    col, tm = place_ref[1], place_ref[2]

    def normed(block):
        return silu_of(block.astype(jnp.float32), mean, scale, gain, shift)

    def put(y, block):
        for j in range(chans // 128):
            plain[j, 16 * y : 16 * y + 16, :] = block[:, 128 * j : 128 * (j + 1)]

    for t in range(4):
        for y in range(10):
            put(y, normed(frame_row(earlier_ref, own_ref, tm, t, y)))
        for x in range(2):
            side[pl.ds(16 * x, 16), :] = normed(border_ref[t, x])
        for dy in range(3):

            def column(x):
                pieces = [plain[j, pl.ds(16 * dy + x, 8, stride=16), :] for j in range(chans // 128)]
                return jnp.concatenate(pieces, axis=1)

            inner = [column(x) for x in range(16)]
            outer = [side[pl.ds(16 * x + dy, 8), :] for x in range(2)]
            left = [jnp.where(col == 0, inner[0], o) for o in outer]
            right = [jnp.where(col == 0, o, inner[15]) for o in outer]
            columns = left + inner + right
            base = t * 160
            for p in range(2):
                for i in range(10 - p):
                    pair = jnp.concatenate([columns[2 * i + p], columns[2 * i + p + 1]], axis=0)
                    out_ref[2 * dy + p, pl.ds(base + 16 * i, 16), :] = pair.astype(jnp.bfloat16)
            out_ref[2 * dy + 1, pl.ds(base + 144, 16), :] = jnp.zeros((16, chans), jnp.bfloat16)


def conv1_kernel(count, bias_ref, copies_ref, gathered_ref, middle_ref, stats_ref, copies, weights, arrived):
    layouts = [pltpu.make_async_copy(copies_ref.at[i], copies.at[i], arrived.at[i]) for i in range(6)]
    fetches = [
        pltpu.make_async_copy(gathered_ref.at[3 * i : 3 * i + 3], weights.at[3 * i : 3 * i + 3], arrived.at[6 + i])
        for i in range(9)
    ]

    def start(dy):
        for copy in [*layouts[2 * dy : 2 * dy + 2], *fetches[dy::3]]:
            copy.start()

    start(0)
    start(1)
    middle_ref[...] = jnp.broadcast_to(bias_ref[...], middle_ref.shape)
    depth = 3 * weights.shape[1]
    for dy in range(3):
        for copy in [*layouts[2 * dy : 2 * dy + 2], *fetches[dy::3]]:
            copy.wait()
        if dy == 0:
            start(2)
        for dt in range(3):
            weight = weights[9 * dt + 3 * dy : 9 * dt + 3 * dy + 3].reshape(depth, weights.shape[2])

            def window(dx, dy=dy, dt=dt):
                starts = [(dt + t) * 160 + (dx // 2) * 16 for t in range(2)]
                return jnp.concatenate([copies[2 * dy + dx % 2, at : at + 144, :] for at in starts], axis=0)

            lhs = jnp.concatenate([window(dx) for dx in range(3)], axis=1)
            middle_ref[...] += jnp.dot(lhs, weight, preferred_element_type=jnp.float32)

    values = middle_ref[...]
    place = lax.broadcasted_iota(jnp.int32, values.shape, 0)
    y, x = place % 8, (place // 8) % 18
    keep = (y >= 1) & (y <= 6) & (x >= 1) & (x <= 16)
    tile = channel_stats(values, keep, count)
    stats_ref[...] = jnp.broadcast_to(tile[None], stats_ref.shape)


def hidden2_kernel(count, peers, place_ref, parts_ref, gain_ref, shift_ref, earlier_ref, middle_ref, copies):
    row, col, tm = place_ref[0], place_ref[1], place_ref[2]
    chans = middle_ref.shape[1]
    tile = merged(parts_ref, count)
    mean, scale = group_moments(tile, count * peers, chans // GROUPS, chans)
    gain, shift = gain_ref[...], shift_ref[...]
    y = lax.broadcasted_iota(jnp.int32, (8, chans), 0)
    for t in range(4):
        if t < 2:
            block = jnp.where(tm == 0, middle_ref[:144, :], earlier_ref[144 * t : 144 * t + 144, :])
        else:
            block = middle_ref[144 * (t - 2) : 144 * (t - 1), :]
        block = silu_of(block, mean, scale, gain, shift)
        columns = [block[8 * x : 8 * x + 8] for x in range(18)]
        columns[0] = jnp.where(col == 0, columns[1], columns[0])
        columns[17] = jnp.where(col == 1, columns[16], columns[17])
        for x in range(18):
            column = columns[x]
            column = jnp.where((y == 0) & (row == 0), pltpu.roll(column, 7, 0), column)
            columns[x] = jnp.where((y == 7) & (row == 7), pltpu.roll(column, 1, 0), column)
        for dy in range(3):
            rolled = columns if dy == 0 else [pltpu.roll(c, 8 - dy, 0) for c in columns]
            for p in range(2):
                for i in range(9 - p):
                    pair = jnp.concatenate([rolled[2 * i + p], rolled[2 * i + p + 1]], axis=0)
                    copies[2 * dy + p, 144 * t + 16 * i : 144 * t + 16 * i + 16, :] = pair.astype(jnp.bfloat16)


def conv2_kernel(copies, bias_ref, features_ref, weight_ref, out_ref, total):
    chans = weight_ref.shape[2]
    rows = [weight_ref[27 + h, 16 * d : 16 * d + 16, :] for d in range(chans // 16) for h in range(2)]
    skip = jnp.concatenate(rows, axis=0)
    shortcut = jnp.dot(features_ref[...], skip, preferred_element_type=jnp.float32) + bias_ref[...]
    for dt in range(3):
        for dy in range(3):
            weight = weight_ref[9 * dt + 3 * dy : 9 * dt + 3 * dy + 3].reshape(3 * chans, chans)
            for t in range(2):

                def window(dx, dy=dy, first=dt + t):
                    start = first * 144 + (dx // 2) * 16
                    return copies[2 * dy + dx % 2, start : start + 128, :]

                lhs = jnp.concatenate([window(dx) for dx in range(3)], axis=1)
                product = jnp.dot(lhs, weight, preferred_element_type=jnp.float32)
                for j in range(chans // 128):
                    part = product[:, 128 * j : 128 * (j + 1)]
                    if dt == 0 and dy == 0:
                        total[j, 128 * t : 128 * t + 128, :] = part
                    else:
                        total[j, 128 * t : 128 * t + 128, :] += part

    for t in range(2):
        for y in range(6):
            conv = [total[j, pl.ds(128 * t + y, 16, stride=8), :] for j in range(chans // 128)]
            at = (6 * t + y) * 16
            out_ref[at : at + 16, :] = (jnp.concatenate(conv, axis=1) + shortcut[at : at + 16]).astype(jnp.bfloat16)


def whole(*_):
    return pl.BlockSpec(memory_space=VMEM)


def per_device(
    features,
    gn1_gain,
    gn1_bias,
    conv1_weight,
    conv1_bias,
    skip_weight,
    gn2_gain,
    gn2_bias,
    conv2_weight,
    conv2_bias,
):
    frames, rows, cols, chans_in = features.shape
    chans_out = conv1_weight.shape[2]
    ntm, nrow, ncol = (lax.axis_size(a) for a in (TM, "row", "col"))
    tm, row, col = (lax.axis_index(a) for a in (TM, "row", "col"))
    place = jnp.stack([row, col, tm]).astype(jnp.int32)
    positions = frames * rows * cols
    plane = nrow * ncol
    flat_features = features.reshape(positions, chans_in)
    tile = jax.ShapeDtypeStruct((8, 128), jnp.float32)

    first = lax.all_gather(conv1_weight, ("row", "col"), axis=1, tiled=True)
    share = conv2_weight.shape[1]
    halves = skip_weight.reshape(2, share, chans_out)
    second = lax.all_gather(jnp.concatenate([conv2_weight, halves], axis=0), ("row", "col"), axis=1, tiled=True)

    def shared(stats, count, beside=()):
        stats = lax.all_to_all(stats, ("row", "col"), 0, 0, tiled=True)
        if beside:
            stats, beside = lax.optimization_barrier((stats, beside))
        stats = pl.pallas_call(
            functools.partial(merge_kernel, count),
            out_shape=jax.ShapeDtypeStruct((ntm, *tile.shape), tile.dtype),
            in_specs=[whole()],
            out_specs=whole(),
        )(stats)
        return lax.all_to_all(stats, TM, 0, 0, tiled=True), beside

    stats = pl.pallas_call(
        stats_kernel,
        out_shape=jax.ShapeDtypeStruct((plane, *tile.shape), tile.dtype),
        in_specs=[whole()],
        out_specs=whole(),
    )(flat_features)
    above = moved(features[:, -2:], "row", 1)
    below = moved(features[:, :2], "row", -1)
    parts, (above, below) = shared(stats, float(positions), (above, below))
    above = jnp.where(row == 0, features[:, :1], above)
    below = jnp.where(row == nrow - 1, features[:, -1:], below)
    own = jnp.concatenate([above, features, below], axis=1)
    earlier = moved(own, TM, 1)
    border = pl.pallas_call(
        border_kernel,
        out_shape=jax.ShapeDtypeStruct((4, 2, 16, chans_in), jnp.bfloat16),
        in_specs=[pl.BlockSpec(memory_space=SMEM)] + [whole()] * 2,
        out_specs=whole(),
        scratch_shapes=[VMEM((chans_in // 128, 288, 128), jnp.float32)],
        compiler_params=pltpu.CompilerParams(vmem_limit_bytes=16 * MIB),
    )(place, earlier, own)
    border = swapped(border, "col")

    copies = pl.pallas_call(
        functools.partial(hidden1_kernel, float(positions * plane), ntm),
        out_shape=jax.ShapeDtypeStruct((6, 640, chans_in), jnp.bfloat16),
        in_specs=[pl.BlockSpec(memory_space=SMEM)] + [whole()] * 6,
        out_specs=whole(),
        scratch_shapes=[VMEM((chans_in // 128, 192, 128), jnp.float32), VMEM((32, chans_in), jnp.float32)],
        compiler_params=pltpu.CompilerParams(vmem_limit_bytes=24 * MIB),
    )(place, parts, gn1_gain[None], gn1_bias[None], earlier, own, border)

    middle, stats = pl.pallas_call(
        functools.partial(conv1_kernel, float(positions)),
        out_shape=(
            jax.ShapeDtypeStruct((288, chans_out), jnp.float32),
            jax.ShapeDtypeStruct((plane, *tile.shape), tile.dtype),
        ),
        in_specs=[whole()] + [pl.BlockSpec(memory_space=HBM)] * 2,
        out_specs=(whole(), whole()),
        scratch_shapes=[
            VMEM(copies.shape, jnp.bfloat16),
            VMEM(first.shape, jnp.bfloat16),
            pltpu.SemaphoreType.DMA((15,)),
        ],
        compiler_params=pltpu.CompilerParams(vmem_limit_bytes=60 * MIB),
    )(conv1_bias[None], copies, first)

    earlier = moved(middle, TM, 1)
    parts, _ = shared(stats, float(positions))

    copies = pl.pallas_call(
        functools.partial(hidden2_kernel, float(positions * plane), ntm),
        out_shape=jax.ShapeDtypeStruct((6, 576, chans_out), jnp.bfloat16),
        in_specs=[pl.BlockSpec(memory_space=SMEM)] + [whole()] * 5,
        out_specs=whole(),
        compiler_params=pltpu.CompilerParams(vmem_limit_bytes=16 * MIB),
    )(place, parts, gn2_gain[None], gn2_bias[None], earlier, middle)

    copies, second = lax.optimization_barrier((copies, second))
    out = pl.pallas_call(
        conv2_kernel,
        out_shape=jax.ShapeDtypeStruct((positions, chans_out), jnp.bfloat16),
        in_specs=[whole()] * 4,
        out_specs=whole(),
        scratch_shapes=[VMEM((chans_out // 128, 272, 128), jnp.float32)],
        compiler_params=pltpu.CompilerParams(vmem_limit_bytes=24 * MIB),
    )(copies, conv2_bias[None], flat_features, second)
    return out.reshape(frames, rows, cols, chans_out)


def solution(mesh):
    mesh = Mesh(mesh.devices.reshape(4, -1, *mesh.devices.shape[1:]), (*TM, "row", "col"))
    in_specs = (
        P(TM, "row", "col", None),
        P(),
        P(),
        P(None, ("row", "col"), None),
        P(),
        P(None, ("row", "col"), None),
        P(),
        P(),
        P(None, ("row", "col"), None),
        P(),
    )
    out_specs = P(TM, "row", "col", None)
    return jax.shard_map(
        per_device, mesh=mesh, in_specs=in_specs, out_specs=out_specs, check_vma=False
    )
```
